256 devices in a mesh: grp: 128 (over x, y, z), rep: 2 (over core).
Axes of the slice: x: 4, y: 4, z: 8, core: 2. Of those that a mesh axis runs over, the one named last changes fastest.
Arguments:
- samples: bfloat16 [1024, 1097728], P(('grp', 'rep')), as said below
- fir_coeffs: float32 [4, 16384], replicated, may hold values from 0.2 to 1
- kept_channels: int32 [256], replicated, may hold values from 0 to 8191, as said below
- usable: int32 [1024], replicated, may hold values 0 or 1
- initial_gains: float32 [256, 2, 1024], P(('grp', 'rep')), as said below
Outputs:
- solved_gains: float32 [256, 2, 1024], P(('grp', 'rep'))
- bandpass: float32 [256, 2, 1024], P(('grp', 'rep'))
The draws below stay inside these ranges and needn't reach their ends.
Inputs may be any that keep to these rules, and one draw needn't show every extreme that they name: Real samples of each input, frame after frame. `kept_channels`: strictly increasing; entry j lies in [j * 32, (j + 1) * 32). `initial_gains`: complex starting gains.
All inputs are finite; a program needn't handle non-finite values.
Results may differ from the reference program's by a relative error of at most 0.004.
Values may be sent and summed in bfloat16 or wider, within the bound.
A program may use at most 128 MiB of HBM per device.

```python
import math
import jax
import jax.numpy as jnp
from jax import lax

INPUTS = 1024
CHAN = 8192
NFFT = 16384
TAPS = 4
SPEC = 64
KEPT = 256
ITERS = 4
POLY = 8


def draw_samples(key, part):
    key = jax.random.fold_in(key, 11)
    keys = jax.random.split(key, 5)
    length = (SPEC + TAPS - 1) * NFFT
    sky = jax.random.normal(keys[0], (length + 1,), jnp.float32)
    amplitude = jnp.exp(jax.random.uniform(keys[1], (INPUTS, 1), jnp.float32, math.log(0.5), math.log(2.0)))
    first_tap = jax.random.uniform(keys[2], (INPUTS, 1), jnp.float32, 0.3, 1.0)
    second_tap = jax.random.uniform(keys[3], (INPUTS, 1), jnp.float32, -0.8, 0.8)
    noise = jax.random.normal(keys[4], (INPUTS, length), jnp.float32)
    signal = amplitude * (first_tap * sky[None, 1:] + second_tap * sky[None, :-1]) + noise
    return signal.astype(jnp.bfloat16)


def draw_kept_channels(key, part):
    key = jax.random.fold_in(key, 23)
    stride = CHAN // KEPT
    offsets = jax.random.randint(key, (KEPT,), 0, stride, jnp.int32)
    position = jnp.arange(KEPT, dtype=jnp.int32)
    offsets = jnp.where(position == 0, 0, jnp.where(position == KEPT - 1, stride - 1, offsets))
    return (position * stride + offsets).astype(jnp.int32)


def draw_initial_gains(key, part):
    key = jax.random.fold_in(key, 37)
    keys = jax.random.split(key, 2)
    common = jax.random.normal(keys[0], (1, 2, INPUTS), jnp.float32) * 0.5
    spread = jax.random.normal(keys[1], (KEPT, 2, INPUTS), jnp.float32) * 0.2
    return (common + spread).astype(jnp.float32)


def plant(entries, key, least, high):
    longest = entries.shape.index(max(entries.shape))
    spots = []
    for shift in (0, 1):
        where = [jax.random.randint(jax.random.fold_in(key, axis), (), 0, length) for axis, length in enumerate(entries.shape)]
        where[longest] = (where[longest] + shift) % entries.shape[longest]
        spots.append(tuple(where))
    return entries.at[spots[0]].set(least).at[spots[1]].set(high)


def setup_inputs(seed: int = 0) -> dict:
    splits = jax.random.split(jax.random.key(seed), 6)
    return {
        "samples": draw_samples(jax.random.fold_in(splits[5], 71), 0),
        "fir_coeffs": jnp.clip(jax.random.uniform(splits[1], (TAPS, NFFT), jnp.float32, 0.2, 1.0), 0.2, 1.0),
        "kept_channels": draw_kept_channels(jax.random.fold_in(splits[5], 71), 0),
        "usable": plant((jax.random.randint(splits[3], (INPUTS,), 0, 16) < 15).astype(jnp.int32), jax.random.fold_in(splits[3], 1), 0, 1),
        "initial_gains": draw_initial_gains(jax.random.fold_in(splits[5], 71), 0),
    }


def legendre_basis(kept_channels):
    coord = kept_channels.astype(jnp.float32) * (2.0 / (CHAN - 1)) - 1.0
    columns = [jnp.ones_like(coord), coord]
    for order in range(1, POLY - 1):
        columns.append(((2 * order + 1) * coord * columns[order] - order * columns[order - 1]) / (order + 1))
    return jnp.stack(columns[:POLY], axis=1)

def solve_gram(gram, moments):
    factor = jnp.linalg.cholesky(gram)
    forward = []
    for row in range(POLY):
        value = moments[row]
        for col in range(row):
            value = value - factor[row, col] * forward[col]
        forward.append(value / factor[row, row])
    backward = [None] * POLY
    for row in range(POLY - 1, -1, -1):
        value = forward[row]
        for col in range(row + 1, POLY):
            value = value - factor[col, row] * backward[col]
        backward[row] = value / factor[row, row]
    return jnp.stack(backward, axis=0)

def calibrate(vis_re, vis_im, power, usable_f, gains):
    scale = lax.rsqrt(power + 1e-06) * usable_f
    weight = scale[:, None] * scale[None, :] * (1.0 - jnp.eye(scale.shape[0], dtype=jnp.float32))
    w_re = vis_re * weight[None]
    w_im = vis_im * weight[None]
    g_re = gains[:, 0]
    g_im = gains[:, 1]
    for step in range(ITERS):
        both = jnp.stack([g_re, g_im], axis=2)
        from_re = jnp.einsum('cpq,cqk->cpk', w_re, both, precision=lax.Precision.HIGHEST)
        from_im = jnp.einsum('cpq,cqk->cpk', w_im, both, precision=lax.Precision.HIGHEST)
        num_re = from_re[:, :, 0] - from_im[:, :, 1]
        num_im = from_re[:, :, 1] + from_im[:, :, 0]
        magnitude = usable_f[None, :] * (g_re * g_re + g_im * g_im)
        total = lax.optimization_barrier(jnp.sum(magnitude, axis=1, keepdims=True))
        denom = total - magnitude + 1e-06
        new_re = num_re / denom
        new_im = num_im / denom
        if step % 2 == 1:
            g_re = (new_re + g_re) / 2.0
            g_im = (new_im + g_im) / 2.0
        else:
            g_re = new_re
            g_im = new_im
    return jnp.stack([g_re, g_im], axis=1)

def reference(samples, fir_coeffs, kept_channels, usable, initial_gains):
    frames_total = SPEC + TAPS - 1
    group = min(64, INPUTS)
    blocks = samples.reshape(INPUTS // group, group, frames_total, NFFT)
    sample_index = jnp.arange(NFFT, dtype=jnp.int32)
    phase = kept_channels.astype(jnp.int32)[:, None] * sample_index[None, :] % NFFT
    angle = phase.astype(jnp.float32) * jnp.float32(2.0 * math.pi / NFFT)
    table_re = jnp.cos(angle).astype(jnp.bfloat16)
    table_im = (-jnp.sin(angle)).astype(jnp.bfloat16)

    def engine(block):
        frames = block.astype(jnp.float32)
        filtered = fir_coeffs[0][None, None, :] * frames[:, 0:SPEC, :]
        for tap in range(1, TAPS):
            filtered = filtered + fir_coeffs[tap][None, None, :] * frames[:, tap:tap + SPEC, :]
        rows = filtered.astype(jnp.bfloat16).reshape(group * SPEC, NFFT)
        spec_re = jnp.dot(rows.astype(jnp.float32), table_re.T.astype(jnp.float32), preferred_element_type=jnp.float32).reshape(group, SPEC, KEPT)
        spec_im = jnp.dot(rows.astype(jnp.float32), table_im.T.astype(jnp.float32), preferred_element_type=jnp.float32).reshape(group, SPEC, KEPT)
        return jnp.stack([spec_re, spec_im], axis=1).astype(jnp.bfloat16)
    spectra = lax.map(engine, blocks).reshape(INPUTS, 2, SPEC, KEPT)
    stacked = jnp.transpose(spectra, (3, 0, 1, 2)).reshape(KEPT, INPUTS, 2 * SPEC)
    squares = stacked.astype(jnp.float32)
    power = lax.optimization_barrier(jnp.sum(lax.optimization_barrier(jnp.sum(squares * squares, axis=2)) / SPEC, axis=0)) / KEPT
    usable_f = usable.astype(jnp.float32)

    def per_channel(pair):
        rows, gains = pair
        other = jnp.concatenate([rows[:, SPEC:], -rows[:, :SPEC]], axis=1)
        vis_re = jnp.dot(rows.astype(jnp.float32), rows.T.astype(jnp.float32), preferred_element_type=jnp.float32) / SPEC
        vis_im = jnp.dot(rows.astype(jnp.float32), other.T.astype(jnp.float32), preferred_element_type=jnp.float32) / SPEC
        return calibrate(vis_re[None], vis_im[None], power, usable_f, gains[None])[0]
    solved = lax.map(per_channel, (stacked, initial_gains))
    basis = legendre_basis(kept_channels)
    gram = jnp.dot(basis.T, basis, precision=lax.Precision.HIGHEST)
    moments = jnp.dot(basis.T, solved.reshape(KEPT, 2 * INPUTS), precision=lax.Precision.HIGHEST)
    coeffs = solve_gram(gram, moments)
    bandpass = jnp.dot(basis, coeffs, precision=lax.Precision.HIGHEST).reshape(KEPT, 2, INPUTS)
    return (solved, bandpass)
```

```python
import math

import jax
import jax.numpy as jnp
from jax import lax
from jax.experimental import pallas as pl
from jax.experimental.pallas import tpu as pltpu
from jax.sharding import PartitionSpec as P

bf, f32 = jnp.bfloat16, jnp.float32
MESH = pl.DeviceIdType.MESH
CHAN = 8192
NFFT = 16384
SPEC = 64
TAPS = 4
FRAMES = SPEC + TAPS - 1
KEPT = 256
INPUTS = 1024
ITERS = 4
POLY = 8
NX, NY, NZ = 4, 4, 8
CHIPS = NX * NY * NZ
PLANE = NX * NY
TILES = NFFT // 128
QT = TILES // 4
CHUNKS = 8
KC = QT // CHUNKS


def turns(phase):
    quad = (phase + NFFT // 8) // (NFFT // 4)
    x = (phase - quad * (NFFT // 4)).astype(f32) * f32(2.0 * math.pi / NFFT)
    x2 = x * x
    s = x * (1.0 + x2 * (-1.0 / 6 + x2 * (1.0 / 120 + x2 * (-1.0 / 5040 + x2 * (1.0 / 362880)))))
    c = 1.0 + x2 * (-0.5 + x2 * (1.0 / 24 + x2 * (-1.0 / 720 + x2 * (1.0 / 40320))))
    odd = (quad & 1) == 1
    cc = jnp.where(odd, s, c)
    ss = jnp.where(odd, c, s)
    cc = jnp.where((quad == 1) | (quad == 2), -cc, cc)
    ss = jnp.where((quad == 2) | (quad == 3), -ss, ss)
    return cc, ss


def loop(f, n):
    def step(i, carry):
        f(i)
        return carry

    lax.fori_loop(0, n, step, 0)


def kernel(
    x_hbm, fir_ref, chan_ref, use_ref, gain_ref,
    solved_ref, band_ref,
    X, Fa, Fb, Ta, Tb, acc, hi, lo, wide, msgs, both, turned,
    pw, pz, pc, sol, splat, part, half, planes, fit, fit_out,
    in_sem, core_send, core_recv, own_sem, turn_send, turn_recv, self_sem,
    pw_send, pw_recv, pz_send, pz_recv, pc_send, pc_recv,
    sol_send, sol_recv, half_send, half_recv, z_send, z_recv, fit_send, fit_recv,
):
    g = lax.axis_index("grp")
    r = lax.axis_index("rep")
    z = lax.rem(g, NZ)
    xy = g // NZ
    y = lax.rem(xy, NY)
    x = xy // NY

    src = x_hbm.reshape(FRAMES, 4, QT, 4, 128)

    def sample_copy(k, j):
        at = pl.ds(KC * k, KC)
        return pltpu.make_async_copy(src.at[:, j, at], X.at[:, at, j], in_sem.at[k, j])

    for k in range(CHUNKS):
        for j in range(4):
            sample_copy(k, j).start()

    def chip_peer(i):
        k, m = i // PLANE, lax.rem(i, PLANE)
        sign = 1 - 2 * lax.rem(k, 2)
        dz = NZ // 2 + sign * ((k + 1) // 2)
        kx, ky = m // NY, lax.rem(m, NY)
        dx = NX // 2 + (1 - 2 * lax.rem(kx, 2)) * ((kx + 1) // 2)
        dy = NY // 2 + (1 - 2 * lax.rem(ky, 2)) * ((ky + 1) // 2)
        px, py, pz = lax.rem(x + dx, NX), lax.rem(y + dy, NY), lax.rem(z + dz, NZ)
        return (px * NY + py) * NZ + pz

    barrier = pltpu.get_barrier_semaphore()
    pl.semaphore_signal(barrier, inc=1, device_id=(g, 1 - r), device_id_type=MESH)
    loop(
        lambda i: pl.semaphore_signal(barrier, inc=1, device_id=(chip_peer(i), r), device_id_type=MESH),
        CHIPS - 1,
    )

    chan = chan_ref[...]

    def table(n0, rows, step):
        n = (lax.broadcasted_iota(jnp.int32, (rows, KEPT), 0) + n0) * step
        return turns((n * chan) & (NFFT - 1))

    c, s = table(0, QT, 128)
    hi[0] = c
    hi[1] = -s

    def low_table(i):
        c, s = table(i * 16, 16, 1)
        at = pl.ds(pl.multiple_of(i * 16, 16), 16)
        lo[0, at, :] = c
        lo[1, at, :] = -s

    loop(low_table, 8)

    rows = X.reshape(FRAMES, QT, 16, 128)
    quarter = lax.broadcasted_iota(jnp.int32, (16, 128), 0) // 4

    def fir(k, h, F, T):
        kk = KC * k + h
        static = isinstance(h, int)
        col = slice(h * 128, h * 128 + 128) if static else pl.ds(pl.multiple_of(h * 128, 128), 128)
        coef = []
        for t in range(TAPS):
            b = [jnp.broadcast_to(fir_ref[j * QT + kk, pl.ds(t, 1)], (16, 128)) for j in range(4)]
            coef.append(
                jnp.where(
                    quarter == 0, b[0], jnp.where(quarter == 1, b[1], jnp.where(quarter == 2, b[2], b[3]))
                )
            )
        w = [rows[f, kk].astype(f32) for f in range(TAPS - 1)]
        for s in range(SPEC):
            w.append(rows[s + TAPS - 1, kk].astype(f32))
            o = coef[0] * w[0] + coef[1] * w[1] + coef[2] * w[2] + coef[3] * w[3]
            F[s * 16 : (s + 1) * 16, col] = o.astype(bf)
            w = w[1:]
        hr, hm = hi[0, pl.ds(kk, 1), :], hi[1, pl.ds(kk, 1), :]
        for q in range(8):
            lr, lm = lo[0, q * 16 : (q + 1) * 16, :], lo[1, q * 16 : (q + 1) * 16, :]
            first = h * 128 + q * 16
            row = slice(first, first + 16) if static else pl.ds(pl.multiple_of(first, 16), 16)
            T[0, row, :] = (hr * lr - hm * lm).astype(bf)
            T[1, row, :] = (hr * lm + hm * lr).astype(bf)

    def mm(F, T):
        for n in range(2):
            d = jnp.dot(F[...], T[n], preferred_element_type=f32)
            for q in range(2):
                acc[2 * n + q] += d[:, q * 128 : (q + 1) * 128]

    def wait_samples(k):
        for j in range(4):
            sample_copy(k, j).wait()

    def stage(k, prev, cur):
        wait_samples(k)
        mm(*prev)
        for h in range(KC):
            fir(k, h, *cur)

    A, B = (Fa, Ta), (Fb, Tb)
    acc[...] = jnp.zeros_like(acc)
    wait_samples(0)
    loop(lambda h: fir(0, h, *A), KC)

    def pair(i):
        stage(2 * i + 1, A, B)
        stage(2 * i + 2, B, A)

    loop(pair, CHUNKS // 2 - 1)
    stage(CHUNKS - 1, A, B)
    mm(*B)

    quads = []
    for j in range(4):
        ph = (chan * j) & 3
        rr = jnp.where(ph == 0, 1.0, jnp.where(ph == 2, -1.0, 0.0))
        ri = jnp.where(ph == 1, -1.0, jnp.where(ph == 3, 1.0, 0.0))
        quads.append((rr, ri))
    sub8 = lax.broadcasted_iota(jnp.int32, (8, 128), 0)
    lane8 = lax.broadcasted_iota(jnp.int32, (8, 128), 1)
    power_row, power_lane = xy // 2, lax.rem(xy, 2) * 64 + z * 8 + r * 4
    powers = jnp.zeros((8, 128), f32)
    for p in range(4):
        sr = si = None
        for j in range(4):
            rr, ri = quads[j]
            at = pl.ds(j * 4 + p, SPEC, stride=16)
            a, b = [jnp.concatenate([acc[q, at, :], acc[q + 1, at, :]], axis=1) for q in (0, 2)]
            tr = rr * a - ri * b if j else a
            ti = rr * b + ri * a if j else b
            sr = tr if sr is None else sr + tr
            si = ti if si is None else si + ti
        v = jnp.concatenate([sr, si], axis=0)
        q = v.astype(bf).astype(f32)
        power = jnp.sum(jnp.sum(q * q, axis=1, keepdims=True), axis=0, keepdims=True)
        powers = jnp.where((sub8 == power_row) & (lane8 == power_lane + p), power, powers)
        wide[pl.ds(p, KEPT, stride=4), :] = v.T
    pw[xy] = powers * f32(1.0 / (SPEC * KEPT))
    pl.semaphore_wait(barrier, CHIPS)

    def send_plane(buf, send, recv):
        def one(i):
            t = lax.rem(xy + 1 + i, PLANE)
            pltpu.make_async_remote_copy(
                src_ref=buf.at[xy], dst_ref=buf.at[xy], send_sem=send, recv_sem=recv,
                device_id=(t * NZ + z, r), device_id_type=MESH,
            ).start()

        loop(one, PLANE - 1)

    def send_z(buf, send, recv):
        def one(i):
            t = lax.rem(z + 1 + i, NZ)
            pltpu.make_async_remote_copy(
                src_ref=buf.at[z], dst_ref=buf.at[z], send_sem=send, recv_sem=recv,
                device_id=(xy * NZ + t, r), device_id_type=MESH,
            ).start()

        loop(one, NZ - 1)

    def drain(buf, n, sem):
        pltpu.make_async_copy(buf.at[pl.ds(0, n)], buf.at[pl.ds(0, n)], sem).wait()

    send_plane(pw, pw_send, pw_recv)

    msgs.reshape(KEPT * 4, 128)[...] = wide[...].astype(bf)
    core_copy = pltpu.make_async_remote_copy(
        src_ref=msgs.at[1 - r], dst_ref=both.at[:, r], send_sem=core_send, recv_sem=core_recv,
        device_id=(g, 1 - r), device_id_type=MESH,
    )
    core_copy.start()
    own_copy = pltpu.make_async_copy(msgs.at[r], both.at[:, r], own_sem)
    own_copy.start()
    own_copy.wait()
    core_copy.wait_recv()

    def send_chip(i):
        t = chip_peer(i)
        pltpu.make_async_remote_copy(
            src_ref=both.at[t], dst_ref=turned.at[g], send_sem=turn_send, recv_sem=turn_recv,
            device_id=(t, r), device_id_type=MESH,
        ).start()

    loop(send_chip, CHIPS - 1)
    self_copy = pltpu.make_async_copy(both.at[g], turned.at[g], self_sem)
    self_copy.start()

    drain(pw, PLANE - 1, pw_recv)
    t = pw[0]
    for i in range(1, PLANE):
        t = t + pw[i]
    pz[z] = t
    send_z(pz, pz_send, pz_recv)

    u = chan.astype(f32) * f32(2.0 / (CHAN - 1)) - 1.0
    poly = [jnp.ones_like(u), u]
    for order in range(1, POLY - 1):
        poly.append(((2 * order + 1) * u * poly[order] - order * poly[order - 1]) / (order + 1))
    sub = lax.broadcasted_iota(jnp.int32, (POLY, KEPT), 0)
    basis = jnp.zeros((POLY, KEPT), f32)
    for k in range(POLY):
        basis = jnp.where(sub == k, jnp.broadcast_to(poly[k], (POLY, KEPT)), basis)
    lane = lax.broadcasted_iota(jnp.int32, (POLY, KEPT), 1)

    def column(q):
        return jnp.sum(jnp.where(lane == q, basis, 0.0), axis=1, keepdims=True)

    aug = jnp.zeros((POLY, 128), f32)
    for k in range(POLY):
        aug = jnp.where(lane8 == k, jnp.sum(basis * poly[k], axis=1, keepdims=True), aug)
    aug = jnp.where(lane8 == POLY, column(r * CHIPS + g), aug)
    aug = jnp.where(lane8 == POLY + 1, column((1 - r) * CHIPS + g), aug)
    for k in range(POLY):
        pivot_row = jnp.sum(jnp.where(sub8 == k, aug, 0.0), axis=0, keepdims=True)
        pivot = jnp.sum(jnp.where(lane8[0:1] == k, pivot_row, 0.0), axis=1, keepdims=True)
        pivot_row = pivot_row / pivot
        factor = jnp.sum(jnp.where(lane8 == k, aug, 0.0), axis=1, keepdims=True)
        aug = jnp.where(sub8 == k, pivot_row, aug - factor * pivot_row)
    for i in range(2):
        v = jnp.sum(jnp.where(lane8 == POLY + i, aug, 0.0), axis=1, keepdims=True)
        splat[PLANE + i] = jnp.broadcast_to(v, (POLY, 128))
    for i in range(PLANE):
        splat[i] = jnp.broadcast_to(column(r * CHIPS + i * NZ + z), (POLY, 128))

    drain(pz, NZ - 1, pz_recv)
    t = pz[0]
    for i in range(1, NZ):
        t = t + pz[i]
    pc[r] = t
    power_copy = pltpu.make_async_remote_copy(
        src_ref=pc.at[r], dst_ref=pc.at[r], send_sem=pc_send, recv_sem=pc_recv,
        device_id=(g, 1 - r), device_id_type=MESH,
    )
    power_copy.start()
    power_copy.wait_recv()
    t = lax.rsqrt(pc[0] + pc[1] + f32(1e-06))
    scale = jnp.concatenate([t[j : j + 1, :] for j in range(8)], axis=1)

    self_copy.wait()
    drain(turned, CHIPS - 1, turn_recv)

    eye = (
        lax.broadcasted_iota(jnp.int32, (128, 128), 0) == lax.broadcasted_iota(jnp.int32, (128, 128), 1)
    ).astype(f32).astype(bf)
    cols = lax.dot_general(
        eye, turned.reshape(INPUTS, 128)[...], (((1,), (1,)), ((), ())), preferred_element_type=f32
    )
    xr, xi = cols[0:SPEC], cols[SPEC : 2 * SPEC]
    use = use_ref[...].astype(f32)
    scale = scale * use
    gr, gi = gain_ref[0:1, :], gain_ref[1:2, :]
    for step in range(ITERS):
        ar, ai = gr * scale, gi * scale
        zr = xr * ar - xi * ai
        zi = xr * ai + xi * ar
        dr = jnp.sum(zr, axis=1, keepdims=True) - zr
        di = jnp.sum(zi, axis=1, keepdims=True) - zi
        nr = jnp.sum(xr * dr + xi * di, axis=0, keepdims=True) * f32(1.0 / SPEC) * scale
        ni = jnp.sum(xr * di - xi * dr, axis=0, keepdims=True) * f32(1.0 / SPEC) * scale
        mag = use * (gr * gr + gi * gi)
        denom = jnp.sum(mag, axis=1, keepdims=True) - mag + f32(1e-06)
        fr, fi = nr / denom, ni / denom
        if step % 2 == 1:
            gr, gi = (fr + gr) * 0.5, (fi + gi) * 0.5
        else:
            gr, gi = fr, fi
    solved_ref[0:1, :] = gr
    solved_ref[1:2, :] = gi
    packed = []
    for v in (gr, gi):
        t = jnp.zeros((8, 128), f32)
        for j in range(8):
            t = jnp.where(sub8 == j, jnp.broadcast_to(v[:, j * 128 : (j + 1) * 128], (8, 128)), t)
        packed.append(t)
    sol[xy] = jnp.concatenate(packed, axis=0)

    send_plane(sol, sol_send, sol_recv)
    drain(sol, PLANE - 1, sol_recv)
    for k in range(POLY):
        m = None
        for i in range(PLANE):
            t = sol[i] * splat[i, k : k + 1, :]
            m = t if m is None else m + t
        part[0, k] = m[0:8]
        part[1, k] = m[8:16]
    half_copy = pltpu.make_async_remote_copy(
        src_ref=part.at[1 - r], dst_ref=half, send_sem=half_send, recv_sem=half_recv,
        device_id=(g, 1 - r), device_id_type=MESH,
    )
    half_copy.start()
    half_copy.wait_recv()
    planes[z] = part[r] + half[...]

    send_z(planes, z_send, z_recv)
    drain(planes, NZ - 1, z_recv)
    mine = theirs = None
    for k in range(POLY):
        m = planes[0, k]
        for i in range(1, NZ):
            m = m + planes[i, k]
        a, b = m * splat[PLANE, k : k + 1, :], m * splat[PLANE + 1, k : k + 1, :]
        mine = a if mine is None else mine + a
        theirs = b if theirs is None else theirs + b
    fit_out[...] = theirs
    fit_copy = pltpu.make_async_remote_copy(
        src_ref=fit_out, dst_ref=fit.at[r], send_sem=fit_send, recv_sem=fit_recv,
        device_id=(g, 1 - r), device_id_type=MESH,
    )
    fit_copy.start()
    fit[r] = mine
    fit_copy.wait_recv()
    for i in range(2):
        for j in range(8):
            band_ref[i : i + 1, j * 128 : (j + 1) * 128] = fit[i, j : j + 1, :]

    core_copy.wait_send()
    drain(both, CHIPS - 1, turn_send)
    drain(pw, PLANE - 1, pw_send)
    drain(pz, NZ - 1, pz_send)
    power_copy.wait_send()
    drain(sol, PLANE - 1, sol_send)
    half_copy.wait_send()
    drain(planes, NZ - 1, z_send)
    fit_copy.wait_send()


def per_device(samples, fir_coeffs, kept_channels, usable, initial_gains):
    tiles = samples.reshape(4, FRAMES * TILES, 128).transpose(1, 0, 2)
    coeffs = fir_coeffs.reshape(TAPS, TILES, 128).transpose(1, 0, 2)
    chan = kept_channels.reshape(CHIPS, 2).T.reshape(1, KEPT)
    vmem = pl.BlockSpec(memory_space=pltpu.VMEM)
    dma = pltpu.SemaphoreType.DMA
    solved, band = pl.pallas_call(
        kernel,
        name="fx_calibrate",
        out_shape=[jax.ShapeDtypeStruct((2, INPUTS), f32)] * 2,
        in_specs=[pl.BlockSpec(memory_space=pl.ANY)] + [vmem] * 4,
        out_specs=[vmem] * 2,
        scratch_shapes=[
            pltpu.VMEM((FRAMES, QT, 4, 4, 128), bf),
            pltpu.VMEM((16 * SPEC, KC * 128), bf),
            pltpu.VMEM((16 * SPEC, KC * 128), bf),
            pltpu.VMEM((2, KC * 128, KEPT), bf),
            pltpu.VMEM((2, KC * 128, KEPT), bf),
            pltpu.VMEM((4, 16 * SPEC, 128), f32),
            pltpu.VMEM((2, QT, KEPT), f32),
            pltpu.VMEM((2, 128, KEPT), f32),
            pltpu.VMEM((4 * KEPT, 128), f32),
            pltpu.VMEM((2, CHIPS, 4, 128), bf),
            pltpu.VMEM((CHIPS, 2, 4, 128), bf),
            pltpu.VMEM((CHIPS, 2, 4, 128), bf),
            pltpu.VMEM((PLANE, 8, 128), f32),
            pltpu.VMEM((NZ, 8, 128), f32),
            pltpu.VMEM((2, 8, 128), f32),
            pltpu.VMEM((PLANE, 16, 128), f32),
            pltpu.VMEM((PLANE + 2, POLY, 128), f32),
            pltpu.VMEM((2, POLY, 8, 128), f32),
            pltpu.VMEM((POLY, 8, 128), f32),
            pltpu.VMEM((NZ, POLY, 8, 128), f32),
            pltpu.VMEM((2, 8, 128), f32),
            pltpu.VMEM((8, 128), f32),
            dma((CHUNKS, 4)),
        ]
        + [dma] * 20,
        compiler_params=pltpu.CompilerParams(
            collective_id=0, has_side_effects=True, vmem_limit_bytes=48 * 2**20
        ),
    )(tiles, coeffs, chan, usable.reshape(1, INPUTS), initial_gains.reshape(2, INPUTS))
    return solved.reshape(1, 2, INPUTS), band.reshape(1, 2, INPUTS)


def solution(mesh):
    placed = (P(("grp", "rep"), None), P(), P(), P(), P(("grp", "rep"), None, None))
    return jax.shard_map(
        per_device,
        mesh=mesh,
        in_specs=placed,
        out_specs=(P(("grp", "rep"), None, None), P(("grp", "rep"), None, None)),
        check_vma=False,
    )
```

```python
import math

import jax
import jax.numpy as jnp
from jax import lax
from jax.experimental import pallas as pl
from jax.experimental.pallas import tpu as pltpu
from jax.sharding import PartitionSpec as P

bf, f32 = jnp.bfloat16, jnp.float32
MESH = pl.DeviceIdType.MESH
CHAN = 8192
NFFT = 16384
SPEC = 64
TAPS = 4
FRAMES = SPEC + TAPS - 1
KEPT = 256
INPUTS = 1024
ITERS = 4
POLY = 8
NX, NY, NZ = 4, 4, 8
CHIPS = NX * NY * NZ
PLANE = NX * NY
TILES = NFFT // 128
QT = TILES // 4
CHUNKS = 8
KC = QT // CHUNKS


def turns(phase):
    quad = (phase + NFFT // 8) // (NFFT // 4)
    x = (phase - quad * (NFFT // 4)).astype(f32) * f32(2.0 * math.pi / NFFT)
    x2 = x * x
    s = x * (1.0 + x2 * (-1.0 / 6 + x2 * (1.0 / 120 + x2 * (-1.0 / 5040 + x2 * (1.0 / 362880)))))
    c = 1.0 + x2 * (-0.5 + x2 * (1.0 / 24 + x2 * (-1.0 / 720 + x2 * (1.0 / 40320))))
    odd = (quad & 1) == 1
    cc = jnp.where(odd, s, c)
    ss = jnp.where(odd, c, s)
    cc = jnp.where((quad == 1) | (quad == 2), -cc, cc)
    ss = jnp.where((quad == 2) | (quad == 3), -ss, ss)
    return cc, ss


def loop(f, n):
    def step(i, carry):
        f(i)
        return carry

    lax.fori_loop(0, n, step, 0)


def kernel(
    x_hbm, fir_hbm, chan_hbm, use_hbm, gain_hbm,
    solved_ref, band_ref,
    X, fir_ref, chan_ref, use_ref, gain_ref,
    Fa, Fb, Ta, Tb, acc, hi, lo, wide, msgs, both, turned,
    pw, pz, mysol, sol, splat, planes, fit, fit_out,
    in_sem, arg_sem, core_send, core_recv, own_sem, turn_send, turn_recv, self_sem,
    pw_send, pw_recv, pz_send, pz_recv,
    sol_send, sol_recv, z_send, z_recv, fit_send, fit_recv, ready,
):
    g = lax.axis_index("grp")
    r = lax.axis_index("rep")
    z = lax.rem(g, NZ)
    xy = g // NZ
    y = lax.rem(xy, NY)
    x = xy // NY

    src = x_hbm.reshape(FRAMES, 4, QT, 4, 128)

    def sample_copy(k, j):
        at = pl.ds(KC * k, KC)
        return pltpu.make_async_copy(src.at[:, j, at], X.at[:, at, j], in_sem.at[k, j])

    args = [
        pltpu.make_async_copy(a, b, arg_sem.at[i])
        for i, (a, b) in enumerate(
            [(chan_hbm, chan_ref), (fir_hbm, fir_ref), (use_hbm, use_ref), (gain_hbm, gain_ref)]
        )
    ]
    args[0].start()
    args[1].start()
    for k in range(CHUNKS):
        for j in range(4):
            sample_copy(k, j).start()
    args[2].start()
    args[3].start()

    barrier = pltpu.get_barrier_semaphore()

    def greet(chip, core):
        pl.semaphore_signal(barrier, inc=1, device_id=(chip, core), device_id_type=MESH)

    def greet_plane(i):
        t = lax.rem(xy * 2 + r + 1 + i, 2 * PLANE)
        greet(t // 2 * NZ + z, lax.rem(t, 2))

    loop(greet_plane, 2 * PLANE - 1)
    loop(lambda i: greet(xy * NZ + lax.rem(z + 1 + i, NZ), r), NZ - 1)

    def plane_is_here():
        pl.semaphore_wait(barrier, 2 * PLANE - 1 + NZ - 1)
        loop(
            lambda i: pl.semaphore_signal(
                ready, inc=1, device_id=(xy * NZ + lax.rem(z + 1 + i, NZ), r), device_id_type=MESH
            ),
            NZ - 1,
        )

    args[0].wait()
    chan = chan_ref[...]

    def table(n0, rows, step):
        n = (lax.broadcasted_iota(jnp.int32, (rows, KEPT), 0) + n0) * step
        return turns((n * chan) & (NFFT - 1))

    c, s = table(0, QT, 128)
    hi[0] = c
    hi[1] = -s

    def low_table(i):
        c, s = table(i * 16, 16, 1)
        at = pl.ds(pl.multiple_of(i * 16, 16), 16)
        lo[0, at, :] = c
        lo[1, at, :] = -s

    loop(low_table, 8)

    rows = X.reshape(FRAMES, QT, 16, 128)
    quarter = lax.broadcasted_iota(jnp.int32, (16, 128), 0) // 4

    def fir(k, h, F, T):
        kk = KC * k + h
        static = isinstance(h, int)
        col = slice(h * 128, h * 128 + 128) if static else pl.ds(pl.multiple_of(h * 128, 128), 128)
        coef = []
        for t in range(TAPS):
            b = [jnp.broadcast_to(fir_ref[j * QT + kk, pl.ds(t, 1)], (16, 128)) for j in range(4)]
            coef.append(
                jnp.where(
                    quarter == 0, b[0], jnp.where(quarter == 1, b[1], jnp.where(quarter == 2, b[2], b[3]))
                )
            )
        w = [rows[f, kk].astype(f32) for f in range(TAPS - 1)]
        for s in range(SPEC):
            w.append(rows[s + TAPS - 1, kk].astype(f32))
            o = coef[0] * w[0] + coef[1] * w[1] + coef[2] * w[2] + coef[3] * w[3]
            F[s * 16 : (s + 1) * 16, col] = o.astype(bf)
            w = w[1:]
        hr, hm = hi[0, pl.ds(kk, 1), :], hi[1, pl.ds(kk, 1), :]
        for q in range(8):
            lr, lm = lo[0, q * 16 : (q + 1) * 16, :], lo[1, q * 16 : (q + 1) * 16, :]
            first = h * 128 + q * 16
            row = slice(first, first + 16) if static else pl.ds(pl.multiple_of(first, 16), 16)
            T[0, row, :] = (hr * lr - hm * lm).astype(bf)
            T[1, row, :] = (hr * lm + hm * lr).astype(bf)

    def mm(F, T):
        for n in range(2):
            d = jnp.dot(F[...], T[n], preferred_element_type=f32)
            for q in range(2):
                acc[2 * n + q] += d[:, q * 128 : (q + 1) * 128]

    def wait_samples(k):
        for j in range(4):
            sample_copy(k, j).wait()

    def stage(k, prev, cur):
        wait_samples(k)
        mm(*prev)
        for h in range(KC):
            fir(k, h, *cur)

    A, B = (Fa, Ta), (Fb, Tb)
    acc[...] = jnp.zeros_like(acc)
    args[1].wait()
    wait_samples(0)
    loop(lambda h: fir(0, h, *A), KC)

    def pair(i):
        pl.when(i == CHUNKS // 2 - 2)(plane_is_here)
        stage(2 * i + 1, A, B)
        stage(2 * i + 2, B, A)

    loop(pair, CHUNKS // 2 - 1)
    stage(CHUNKS - 1, A, B)
    mm(*B)

    quads = []
    for j in range(4):
        ph = (chan * j) & 3
        rr = jnp.where(ph == 0, 1.0, jnp.where(ph == 2, -1.0, 0.0))
        ri = jnp.where(ph == 1, -1.0, jnp.where(ph == 3, 1.0, 0.0))
        quads.append((rr, ri))
    sub8 = lax.broadcasted_iota(jnp.int32, (8, 128), 0)
    lane8 = lax.broadcasted_iota(jnp.int32, (8, 128), 1)
    power_row, power_lane = xy // 2, lax.rem(xy, 2) * 64 + z * 8 + r * 4
    powers = jnp.zeros((8, 128), f32)
    spectra = []
    for p in range(4):
        sr = si = None
        for j in range(4):
            rr, ri = quads[j]
            at = pl.ds(j * 4 + p, SPEC, stride=16)
            a, b = [jnp.concatenate([acc[q, at, :], acc[q + 1, at, :]], axis=1) for q in (0, 2)]
            tr = rr * a - ri * b if j else a
            ti = rr * b + ri * a if j else b
            sr = tr if sr is None else sr + tr
            si = ti if si is None else si + ti
        v = jnp.concatenate([sr, si], axis=0)
        q = v.astype(bf).astype(f32)
        power = jnp.sum(jnp.sum(q * q, axis=1, keepdims=True), axis=0, keepdims=True)
        powers = jnp.where((sub8 == power_row) & (lane8 == power_lane + p), power, powers)
        spectra.append(v)
    pw[xy * 2 + r] = powers * f32(1.0 / (SPEC * KEPT))
    pl.semaphore_wait(ready, NZ - 1)

    def send_plane(source, buf, send, recv):
        def one(i):
            t = lax.rem(xy * 2 + r + 1 + i, 2 * PLANE)
            core = lax.rem(t, 2)
            pltpu.make_async_remote_copy(
                src_ref=source(core), dst_ref=buf.at[xy * 2 + r], send_sem=send, recv_sem=recv,
                device_id=(t // 2 * NZ + z, core), device_id_type=MESH,
            ).start()

        loop(one, 2 * PLANE - 1)

    def send_z(buf, send, recv):
        def one(i):
            t = lax.rem(z + 1 + i, NZ)
            pltpu.make_async_remote_copy(
                src_ref=buf.at[z], dst_ref=buf.at[z], send_sem=send, recv_sem=recv,
                device_id=(xy * NZ + t, r), device_id_type=MESH,
            ).start()

        loop(one, NZ - 1)

    def drain(buf, n, sem):
        pltpu.make_async_copy(buf.at[pl.ds(0, n)], buf.at[pl.ds(0, n)], sem).wait()

    send_plane(lambda core: pw.at[xy * 2 + r], pw, pw_send, pw_recv)

    for p in range(4):
        wide[pl.ds(p, KEPT, stride=4), :] = spectra[p].T
    msgs.reshape(KEPT * 4, 128)[...] = wide[...].astype(bf)
    core_copy = pltpu.make_async_remote_copy(
        src_ref=msgs.at[:, 1 - r], dst_ref=both.at[:, r], send_sem=core_send, recv_sem=core_recv,
        device_id=(g, 1 - r), device_id_type=MESH,
    )
    core_copy.start()
    own_copy = pltpu.make_async_copy(msgs.at[:, r], both.at[:, r], own_sem)
    own_copy.start()
    own_copy.wait()
    core_copy.wait_recv()

    def send_chip(t):
        pltpu.make_async_remote_copy(
            src_ref=both.at[t], dst_ref=turned.at[g], send_sem=turn_send, recv_sem=turn_recv,
            device_id=(t, r), device_id_type=MESH,
        ).start()

    def send_level(k):
        pz_ = lax.rem(z + NZ // 2 + (1 - 2 * lax.rem(k, 2)) * ((k + 1) // 2), NZ)
        for m in range(PLANE):
            send_chip(lax.rem(xy + PLANE // 2 + m, PLANE) * NZ + pz_)

    loop(send_level, NZ - 1)
    for m in range(1, PLANE):
        send_chip(lax.rem(xy + m, PLANE) * NZ + z)
    self_copy = pltpu.make_async_copy(both.at[g], turned.at[g], self_sem)
    self_copy.start()

    drain(pw, 2 * PLANE - 1, pw_recv)
    t = pw[0]
    for i in range(1, 2 * PLANE):
        t = t + pw[i]
    pz[z] = t
    send_z(pz, pz_send, pz_recv)

    u = chan.astype(f32) * f32(2.0 / (CHAN - 1)) - 1.0
    poly = [jnp.ones_like(u), u]
    for order in range(1, POLY - 1):
        poly.append(((2 * order + 1) * u * poly[order] - order * poly[order - 1]) / (order + 1))
    sub = lax.broadcasted_iota(jnp.int32, (POLY, KEPT), 0)
    basis = jnp.zeros((POLY, KEPT), f32)
    for k in range(POLY):
        basis = jnp.where(sub == k, jnp.broadcast_to(poly[k], (POLY, KEPT)), basis)
    lane = lax.broadcasted_iota(jnp.int32, (POLY, KEPT), 1)

    def column(q):
        return jnp.sum(jnp.where(lane == q, basis, 0.0), axis=1, keepdims=True)

    aug = jnp.zeros((POLY, 128), f32)
    for k in range(POLY):
        aug = jnp.where(lane8 == k, jnp.sum(basis * poly[k], axis=1, keepdims=True), aug)
    aug = jnp.where(lane8 == POLY, column(2 * g + r), aug)
    aug = jnp.where(lane8 == POLY + 1, column(2 * g + 1 - r), aug)
    for k in range(POLY):
        pivot_row = jnp.sum(jnp.where(sub8 == k, aug, 0.0), axis=0, keepdims=True)
        pivot = jnp.sum(jnp.where(lane8[0:1] == k, pivot_row, 0.0), axis=1, keepdims=True)
        pivot_row = pivot_row / pivot
        factor = jnp.sum(jnp.where(lane8 == k, aug, 0.0), axis=1, keepdims=True)
        aug = jnp.where(sub8 == k, pivot_row, aug - factor * pivot_row)
    for i in range(2):
        v = jnp.sum(jnp.where(lane8 == POLY + i, aug, 0.0), axis=1, keepdims=True)
        splat[2 * PLANE + i] = jnp.broadcast_to(v, (POLY, 128))
    for i in range(2 * PLANE):
        splat[i] = jnp.broadcast_to(column(i // 2 * (2 * NZ) + z * 2 + i % 2), (POLY, 128))

    drain(pz, NZ - 1, pz_recv)
    t = pz[0]
    for i in range(1, NZ):
        t = t + pz[i]
    t = lax.rsqrt(t + f32(1e-06))
    scale = jnp.concatenate([t[j : j + 1, :] for j in range(8)], axis=1)

    args[2].wait()
    args[3].wait()
    self_copy.wait()
    drain(turned, CHIPS - 1, turn_recv)

    eye = (
        lax.broadcasted_iota(jnp.int32, (128, 128), 0) == lax.broadcasted_iota(jnp.int32, (128, 128), 1)
    ).astype(f32).astype(bf)
    cols = lax.dot_general(
        eye, turned.reshape(INPUTS, 128)[...], (((1,), (1,)), ((), ())), preferred_element_type=f32
    )
    xr, xi = cols[0:SPEC], cols[SPEC : 2 * SPEC]
    use = use_ref[...].astype(f32)
    scale = scale * use
    gr, gi = gain_ref[0:1, :], gain_ref[1:2, :]
    for step in range(ITERS):
        ar, ai = gr * scale, gi * scale
        zr = xr * ar - xi * ai
        zi = xr * ai + xi * ar
        dr = jnp.sum(zr, axis=1, keepdims=True) - zr
        di = jnp.sum(zi, axis=1, keepdims=True) - zi
        nr = jnp.sum(xr * dr + xi * di, axis=0, keepdims=True) * f32(1.0 / SPEC) * scale
        ni = jnp.sum(xr * di - xi * dr, axis=0, keepdims=True) * f32(1.0 / SPEC) * scale
        mag = use * (gr * gr + gi * gi)
        denom = jnp.sum(mag, axis=1, keepdims=True) - mag + f32(1e-06)
        fr, fi = nr / denom, ni / denom
        if step % 2 == 1:
            gr, gi = (fr + gr) * 0.5, (fi + gi) * 0.5
        else:
            gr, gi = fr, fi
    solved_ref[0:1, :] = gr
    solved_ref[1:2, :] = gi
    for i, v in enumerate((gr, gi)):
        t = jnp.zeros((8, 128), f32)
        for j in range(8):
            t = jnp.where(sub8 == j, jnp.broadcast_to(v[:, j * 128 : (j + 1) * 128], (8, 128)), t)
        mysol[i] = t

    send_plane(lambda core: mysol.at[core], sol, sol_send, sol_recv)
    sol[xy * 2 + r] = mysol[r]
    drain(sol, 2 * PLANE - 1, sol_recv)
    part = []
    for k in range(POLY):
        m = None
        for i in range(2 * PLANE):
            t = sol[i] * splat[i, k : k + 1, :]
            m = t if m is None else m + t
        part.append(m)
    part = jnp.concatenate(part, axis=0)
    sent = part.astype(bf)
    planes[z] = sent
    send_z(planes, z_send, z_recv)
    total = part - sent.astype(f32)
    drain(planes, NZ - 1, z_recv)
    for i in range(NZ):
        total = total + planes[i].astype(f32)
    mine = theirs = None
    for k in range(POLY):
        m = total[8 * k : 8 * (k + 1)]
        a, b = m * splat[2 * PLANE, k : k + 1, :], m * splat[2 * PLANE + 1, k : k + 1, :]
        mine = a if mine is None else mine + a
        theirs = b if theirs is None else theirs + b
    fit_out[...] = theirs
    fit_copy = pltpu.make_async_remote_copy(
        src_ref=fit_out, dst_ref=fit.at[r], send_sem=fit_send, recv_sem=fit_recv,
        device_id=(g, 1 - r), device_id_type=MESH,
    )
    fit_copy.start()
    fit[r] = mine
    fit_copy.wait_recv()
    for i in range(2):
        for j in range(8):
            band_ref[i : i + 1, j * 128 : (j + 1) * 128] = fit[i, j : j + 1, :]

    core_copy.wait_send()
    drain(both, CHIPS - 1, turn_send)
    drain(pw, 2 * PLANE - 1, pw_send)
    drain(pz, NZ - 1, pz_send)
    drain(sol, 2 * PLANE - 1, sol_send)
    drain(planes, NZ - 1, z_send)
    fit_copy.wait_send()


def per_device(samples, fir_coeffs, kept_channels, usable, initial_gains):
    tiles = samples.reshape(4, FRAMES * TILES, 128).transpose(1, 0, 2)
    coeffs = fir_coeffs.reshape(TAPS, TILES, 128).transpose(1, 0, 2)
    chan = kept_channels.reshape(1, KEPT)
    vmem = pl.BlockSpec(memory_space=pltpu.VMEM)
    dma = pltpu.SemaphoreType.DMA
    solved, band = pl.pallas_call(
        kernel,
        name="fx_calibrate",
        out_shape=[jax.ShapeDtypeStruct((2, INPUTS), f32)] * 2,
        in_specs=[pl.BlockSpec(memory_space=pltpu.HBM)] * 5,
        out_specs=[vmem] * 2,
        scratch_shapes=[
            pltpu.VMEM((FRAMES, QT, 4, 4, 128), bf),
            pltpu.VMEM((TILES, TAPS, 128), f32),
            pltpu.VMEM((1, KEPT), jnp.int32),
            pltpu.VMEM((1, INPUTS), jnp.int32),
            pltpu.VMEM((2, INPUTS), f32),
            pltpu.VMEM((16 * SPEC, KC * 128), bf),
            pltpu.VMEM((16 * SPEC, KC * 128), bf),
            pltpu.VMEM((2, KC * 128, KEPT), bf),
            pltpu.VMEM((2, KC * 128, KEPT), bf),
            pltpu.VMEM((4, 16 * SPEC, 128), f32),
            pltpu.VMEM((2, QT, KEPT), f32),
            pltpu.VMEM((2, 128, KEPT), f32),
            pltpu.VMEM((4 * KEPT, 128), f32),
            pltpu.VMEM((CHIPS, 2, 4, 128), bf),
            pltpu.VMEM((CHIPS, 2, 4, 128), bf),
            pltpu.VMEM((CHIPS, 2, 4, 128), bf),
            pltpu.VMEM((2 * PLANE, 8, 128), f32),
            pltpu.VMEM((NZ, 8, 128), f32),
            pltpu.VMEM((2, 8, 128), f32),
            pltpu.VMEM((2 * PLANE, 8, 128), f32),
            pltpu.VMEM((2 * PLANE + 2, POLY, 128), f32),
            pltpu.VMEM((NZ, POLY * 8, 128), bf),
            pltpu.VMEM((2, 8, 128), f32),
            pltpu.VMEM((8, 128), f32),
            dma((CHUNKS, 4)),
            dma((4,)),
        ]
        + [dma] * 16
        + [pltpu.SemaphoreType.REGULAR],
        compiler_params=pltpu.CompilerParams(
            collective_id=0, has_side_effects=True, vmem_limit_bytes=60 * 2**20
        ),
    )(tiles, coeffs, chan, usable.reshape(1, INPUTS), initial_gains.reshape(2, INPUTS))
    return solved.reshape(1, 2, INPUTS), band.reshape(1, 2, INPUTS)


def solution(mesh):
    placed = (P(("grp", "rep"), None), P(), P(), P(), P(("grp", "rep"), None, None))
    return jax.shard_map(
        per_device,
        mesh=mesh,
        in_specs=placed,
        out_specs=(P(("grp", "rep"), None, None), P(("grp", "rep"), None, None)),
        check_vma=False,
    )
```

```python
import math

import jax
import jax.numpy as jnp
from jax import lax
from jax.experimental import pallas as pl
from jax.experimental.pallas import tpu as pltpu
from jax.sharding import PartitionSpec as P

bf, f32 = jnp.bfloat16, jnp.float32
MESH = pl.DeviceIdType.MESH
CHAN = 8192
NFFT = 16384
SPEC = 64
TAPS = 4
FRAMES = SPEC + TAPS - 1
KEPT = 256
INPUTS = 1024
ITERS = 4
POLY = 8
NX, NY, NZ = 4, 4, 8
CHIPS = NX * NY * NZ
PLANE = NX * NY
TILES = NFFT // 128
QT = TILES // 4
CHUNKS = 8
KC = QT // CHUNKS


def turns(phase):
    quad = (phase + NFFT // 8) // (NFFT // 4)
    x = (phase - quad * (NFFT // 4)).astype(f32) * f32(2.0 * math.pi / NFFT)
    x2 = x * x
    s = x * (1.0 + x2 * (-1.0 / 6 + x2 * (1.0 / 120 + x2 * (-1.0 / 5040 + x2 * (1.0 / 362880)))))
    c = 1.0 + x2 * (-0.5 + x2 * (1.0 / 24 + x2 * (-1.0 / 720 + x2 * (1.0 / 40320))))
    odd = (quad & 1) == 1
    cc = jnp.where(odd, s, c)
    ss = jnp.where(odd, c, s)
    cc = jnp.where((quad == 1) | (quad == 2), -cc, cc)
    ss = jnp.where((quad == 2) | (quad == 3), -ss, ss)
    return cc, ss


def far_first(n):
    return sorted(range(n), key=lambda d: -min(d, n - d))


PLANE_ORDER = sorted(
    ((dx, dy) for dx in range(NX) for dy in range(NY)),
    key=lambda d: -min(d[0], NX - d[0]) - min(d[1], NY - d[1]),
)


def loop(f, n):
    def step(i, carry):
        f(i)
        return carry

    lax.fori_loop(0, n, step, 0)


def kernel(
    x_hbm, fir_hbm, chan_hbm, use_hbm, gain_hbm,
    solved_ref, band_ref,
    X, fir_ref, chan_ref, use_ref, gain_ref,
    Fa, Fb, Ta, Tb, acc, hi, lo, wide, msgs, turned,
    pw, pz, mysol, sol, splat, planes, fit, fit_out,
    in_sem, arg_sem, turn_send, turn_recv, self_sem,
    pw_send, pw_recv, pz_send, pz_recv,
    sol_send, sol_recv, z_send, z_recv, fit_send, fit_recv, ready,
):
    g = lax.axis_index("grp")
    r = lax.axis_index("rep")
    z = lax.rem(g, NZ)
    xy = g // NZ
    y = lax.rem(xy, NY)
    x = xy // NY

    src = x_hbm.reshape(FRAMES, 4, QT, 4, 128)

    def sample_copy(k, j):
        at = pl.ds(KC * k, KC)
        return pltpu.make_async_copy(src.at[:, j, at], X.at[:, at, j], in_sem.at[k, j])

    args = [
        pltpu.make_async_copy(a, b, arg_sem.at[i])
        for i, (a, b) in enumerate(
            [(chan_hbm, chan_ref), (fir_hbm, fir_ref), (use_hbm, use_ref), (gain_hbm, gain_ref)]
        )
    ]
    args[0].start()
    args[1].start()
    for k in range(CHUNKS):
        for j in range(4):
            sample_copy(k, j).start()
    args[2].start()
    args[3].start()

    barrier = pltpu.get_barrier_semaphore()

    def greet(chip, core):
        pl.semaphore_signal(barrier, inc=1, device_id=(chip, core), device_id_type=MESH)

    def plane_chips():
        return [lax.rem(x + dx, NX) * NY + lax.rem(y + dy, NY) for dx, dy in PLANE_ORDER]

    for t in plane_chips()[:-1]:
        greet(t * NZ + z, 0)
        greet(t * NZ + z, 1)
    greet(g, 1 - r)
    for d in far_first(NZ)[:-1]:
        greet(xy * NZ + lax.rem(z + d, NZ), r)

    def plane_is_here():
        pl.semaphore_wait(barrier, 2 * PLANE - 1 + NZ - 1)
        for d in far_first(NZ)[:-1]:
            pl.semaphore_signal(
                ready, inc=1, device_id=(xy * NZ + lax.rem(z + d, NZ), r), device_id_type=MESH
            )

    args[0].wait()
    chan = chan_ref[...]

    def table(n0, rows, step):
        n = (lax.broadcasted_iota(jnp.int32, (rows, KEPT), 0) + n0) * step
        return turns((n * chan) & (NFFT - 1))

    c, s = table(0, QT, 128)
    hi[0] = c
    hi[1] = -s

    def low_table(i):
        c, s = table(i * 16, 16, 1)
        at = pl.ds(pl.multiple_of(i * 16, 16), 16)
        lo[0, at, :] = c
        lo[1, at, :] = -s

    loop(low_table, 8)

    rows = X.reshape(FRAMES, QT, 16, 128)
    quarter = lax.broadcasted_iota(jnp.int32, (16, 128), 0) // 4

    def fir(k, h, F, T):
        kk = KC * k + h
        static = isinstance(h, int)
        col = slice(h * 128, h * 128 + 128) if static else pl.ds(pl.multiple_of(h * 128, 128), 128)
        coef = []
        for t in range(TAPS):
            b = [jnp.broadcast_to(fir_ref[j * QT + kk, pl.ds(t, 1)], (16, 128)) for j in range(4)]
            coef.append(
                jnp.where(
                    quarter == 0, b[0], jnp.where(quarter == 1, b[1], jnp.where(quarter == 2, b[2], b[3]))
                )
            )
        w = [rows[f, kk].astype(f32) for f in range(TAPS - 1)]
        for s in range(SPEC):
            w.append(rows[s + TAPS - 1, kk].astype(f32))
            o = coef[0] * w[0] + coef[1] * w[1] + coef[2] * w[2] + coef[3] * w[3]
            F[s * 16 : (s + 1) * 16, col] = o.astype(bf)
            w = w[1:]
        hr, hm = hi[0, pl.ds(kk, 1), :], hi[1, pl.ds(kk, 1), :]
        for q in range(8):
            lr, lm = lo[0, q * 16 : (q + 1) * 16, :], lo[1, q * 16 : (q + 1) * 16, :]
            first = h * 128 + q * 16
            row = slice(first, first + 16) if static else pl.ds(pl.multiple_of(first, 16), 16)
            T[0, row, :] = (hr * lr - hm * lm).astype(bf)
            T[1, row, :] = (hr * lm + hm * lr).astype(bf)

    def mm(F, T):
        for n in range(2):
            d = jnp.dot(F[...], T[n], preferred_element_type=f32)
            for q in range(2):
                acc[2 * n + q] += d[:, q * 128 : (q + 1) * 128]

    def wait_samples(k):
        for j in range(4):
            sample_copy(k, j).wait()

    def stage(k, prev, cur):
        wait_samples(k)
        mm(*prev)
        for h in range(KC):
            fir(k, h, *cur)

    A, B = (Fa, Ta), (Fb, Tb)
    acc[...] = jnp.zeros_like(acc)
    args[1].wait()
    wait_samples(0)
    loop(lambda h: fir(0, h, *A), KC)

    def pair(i):
        pl.when(i == CHUNKS // 2 - 2)(plane_is_here)
        stage(2 * i + 1, A, B)
        stage(2 * i + 2, B, A)

    loop(pair, CHUNKS // 2 - 1)
    stage(CHUNKS - 1, A, B)
    mm(*B)

    quads = []
    for j in range(4):
        ph = (chan * j) & 3
        rr = jnp.where(ph == 0, 1.0, jnp.where(ph == 2, -1.0, 0.0))
        ri = jnp.where(ph == 1, -1.0, jnp.where(ph == 3, 1.0, 0.0))
        quads.append((rr, ri))
    sub8 = lax.broadcasted_iota(jnp.int32, (8, 128), 0)
    lane8 = lax.broadcasted_iota(jnp.int32, (8, 128), 1)
    power_row, power_lane = xy // 2, lax.rem(xy, 2) * 64 + z * 8 + r * 4
    powers = jnp.zeros((8, 128), f32)
    spectra = []
    for p in range(4):
        sr = si = None
        for j in range(4):
            rr, ri = quads[j]
            at = pl.ds(j * 4 + p, SPEC, stride=16)
            a, b = [jnp.concatenate([acc[q, at, :], acc[q + 1, at, :]], axis=1) for q in (0, 2)]
            tr = rr * a - ri * b if j else a
            ti = rr * b + ri * a if j else b
            sr = tr if sr is None else sr + tr
            si = ti if si is None else si + ti
        v = jnp.concatenate([sr, si], axis=0)
        q = v.astype(bf).astype(f32)
        power = jnp.sum(jnp.sum(q * q, axis=1, keepdims=True), axis=0, keepdims=True)
        powers = jnp.where((sub8 == power_row) & (lane8 == power_lane + p), power, powers)
        spectra.append(v)
    pz[z] = powers * f32(1.0 / (SPEC * KEPT))
    pl.semaphore_wait(ready, NZ - 1)

    def send_plane(source, buf, send, recv):
        def one(chip, core):
            pltpu.make_async_remote_copy(
                src_ref=source(core), dst_ref=buf.at[xy * 2 + r], send_sem=send, recv_sem=recv,
                device_id=(chip, core), device_id_type=MESH,
            ).start()

        for t in plane_chips()[:-1]:
            one(t * NZ + z, 0)
            one(t * NZ + z, 1)
        one(g, 1 - r)

    def send_z(buf, send, recv):
        for d in far_first(NZ)[:-1]:
            pltpu.make_async_remote_copy(
                src_ref=buf.at[z], dst_ref=buf.at[z], send_sem=send, recv_sem=recv,
                device_id=(xy * NZ + lax.rem(z + d, NZ), r), device_id_type=MESH,
            ).start()

    def drain(buf, n, sem):
        pltpu.make_async_copy(buf.at[pl.ds(0, n)], buf.at[pl.ds(0, n)], sem).wait()

    send_z(pz, pz_send, pz_recv)

    for p in range(4):
        wide[pl.ds(p, KEPT, stride=4), :] = spectra[p].T
    msgs.reshape(KEPT * 4, 128)[...] = wide[...].astype(bf)
    me = 2 * g + r

    def send_block(t):
        pltpu.make_async_remote_copy(
            src_ref=msgs.at[t], dst_ref=turned.at[me], send_sem=turn_send, recv_sem=turn_recv,
            device_id=(t // 2, lax.rem(t, 2)), device_id_type=MESH,
        ).start()

    def send_chip(t):
        for core in range(2):
            pltpu.make_async_remote_copy(
                src_ref=msgs.at[2 * t + core], dst_ref=turned.at[me], send_sem=turn_send, recv_sem=turn_recv,
                device_id=(t, core), device_id_type=MESH,
            ).start()

    def send_level(k):
        far = lax.rem(z + NZ // 2 + (1 - 2 * lax.rem(k, 2)) * ((k + 1) // 2), NZ)
        for m in range(PLANE):
            send_chip(lax.rem(xy + PLANE // 2 + m, PLANE) * NZ + far)

    loop(send_level, NZ - 2)

    drain(pz, NZ - 1, pz_recv)
    t = pz[0]
    for i in range(1, NZ):
        t = t + pz[i]
    pw[xy * 2 + r] = t
    send_plane(lambda core: pw.at[xy * 2 + r], pw, pw_send, pw_recv)

    send_level(NZ - 2)
    for m in range(1, PLANE):
        send_chip(lax.rem(xy + m, PLANE) * NZ + z)
    send_block(2 * g + 1 - r)
    self_copy = pltpu.make_async_copy(msgs.at[me], turned.at[me], self_sem)
    self_copy.start()

    u = chan.astype(f32) * f32(2.0 / (CHAN - 1)) - 1.0
    poly = [jnp.ones_like(u), u]
    for order in range(1, POLY - 1):
        poly.append(((2 * order + 1) * u * poly[order] - order * poly[order - 1]) / (order + 1))
    sub = lax.broadcasted_iota(jnp.int32, (POLY, KEPT), 0)
    basis = jnp.zeros((POLY, KEPT), f32)
    for k in range(POLY):
        basis = jnp.where(sub == k, jnp.broadcast_to(poly[k], (POLY, KEPT)), basis)
    lane = lax.broadcasted_iota(jnp.int32, (POLY, KEPT), 1)

    def column(q):
        return jnp.sum(jnp.where(lane == q, basis, 0.0), axis=1, keepdims=True)

    aug = jnp.zeros((POLY, 128), f32)
    for k in range(POLY):
        aug = jnp.where(lane8 == k, jnp.sum(basis * poly[k], axis=1, keepdims=True), aug)
    aug = jnp.where(lane8 == POLY, column(2 * g + r), aug)
    aug = jnp.where(lane8 == POLY + 1, column(2 * g + 1 - r), aug)
    for k in range(POLY):
        pivot_row = jnp.sum(jnp.where(sub8 == k, aug, 0.0), axis=0, keepdims=True)
        pivot = jnp.sum(jnp.where(lane8[0:1] == k, pivot_row, 0.0), axis=1, keepdims=True)
        pivot_row = pivot_row / pivot
        factor = jnp.sum(jnp.where(lane8 == k, aug, 0.0), axis=1, keepdims=True)
        aug = jnp.where(sub8 == k, pivot_row, aug - factor * pivot_row)
    for i in range(2):
        v = jnp.sum(jnp.where(lane8 == POLY + i, aug, 0.0), axis=1, keepdims=True)
        splat[2 * PLANE + i] = jnp.broadcast_to(v, (POLY, 128))
    for i in range(2 * PLANE):
        splat[i] = jnp.broadcast_to(column(i // 2 * (2 * NZ) + z * 2 + i % 2), (POLY, 128))

    drain(pw, 2 * PLANE - 1, pw_recv)
    t = pw[0]
    for i in range(1, 2 * PLANE):
        t = t + pw[i]
    t = lax.rsqrt(t + f32(1e-06))
    scale = jnp.concatenate([t[j : j + 1, :] for j in range(8)], axis=1)

    args[2].wait()
    args[3].wait()
    self_copy.wait()
    drain(turned, 2 * CHIPS - 1, turn_recv)

    eye = (
        lax.broadcasted_iota(jnp.int32, (128, 128), 0) == lax.broadcasted_iota(jnp.int32, (128, 128), 1)
    ).astype(f32).astype(bf)
    cols = lax.dot_general(
        eye, turned.reshape(INPUTS, 128)[...], (((1,), (1,)), ((), ())), preferred_element_type=f32
    )
    xr, xi = cols[0:SPEC], cols[SPEC : 2 * SPEC]
    use = use_ref[...].astype(f32)
    scale = scale * use
    gr, gi = gain_ref[0:1, :], gain_ref[1:2, :]
    for step in range(ITERS):
        ar, ai = gr * scale, gi * scale
        zr = xr * ar - xi * ai
        zi = xr * ai + xi * ar
        dr = jnp.sum(zr, axis=1, keepdims=True) - zr
        di = jnp.sum(zi, axis=1, keepdims=True) - zi
        nr = jnp.sum(xr * dr + xi * di, axis=0, keepdims=True) * f32(1.0 / SPEC) * scale
        ni = jnp.sum(xr * di - xi * dr, axis=0, keepdims=True) * f32(1.0 / SPEC) * scale
        mag = use * (gr * gr + gi * gi)
        denom = jnp.sum(mag, axis=1, keepdims=True) - mag + f32(1e-06)
        fr, fi = nr / denom, ni / denom
        if step % 2 == 1:
            gr, gi = (fr + gr) * 0.5, (fi + gi) * 0.5
        else:
            gr, gi = fr, fi
    solved_ref[0:1, :] = gr
    solved_ref[1:2, :] = gi
    for i, v in enumerate((gr, gi)):
        t = jnp.zeros((8, 128), f32)
        for j in range(8):
            t = jnp.where(sub8 == j, jnp.broadcast_to(v[:, j * 128 : (j + 1) * 128], (8, 128)), t)
        mysol[i] = t.astype(bf)

    send_plane(lambda core: mysol.at[core], sol, sol_send, sol_recv)
    sol[xy * 2 + r] = mysol[r]
    drain(sol, 2 * PLANE - 1, sol_recv)
    part = []
    for k in range(POLY):
        m = None
        for i in range(2 * PLANE):
            t = sol[i].astype(f32) * splat[i, k : k + 1, :]
            m = t if m is None else m + t
        part.append(m)
    part = jnp.concatenate(part, axis=0)
    sent = part.astype(bf)
    planes[z] = sent
    send_z(planes, z_send, z_recv)
    total = part - sent.astype(f32)
    drain(planes, NZ - 1, z_recv)
    for i in range(NZ):
        total = total + planes[i].astype(f32)
    mine = theirs = None
    for k in range(POLY):
        m = total[8 * k : 8 * (k + 1)]
        a, b = m * splat[2 * PLANE, k : k + 1, :], m * splat[2 * PLANE + 1, k : k + 1, :]
        mine = a if mine is None else mine + a
        theirs = b if theirs is None else theirs + b
    fit_out[...] = theirs
    fit_copy = pltpu.make_async_remote_copy(
        src_ref=fit_out, dst_ref=fit.at[r], send_sem=fit_send, recv_sem=fit_recv,
        device_id=(g, 1 - r), device_id_type=MESH,
    )
    fit_copy.start()
    fit[r] = mine
    fit_copy.wait_recv()
    for i in range(2):
        for j in range(8):
            band_ref[i : i + 1, j * 128 : (j + 1) * 128] = fit[i, j : j + 1, :]

    drain(msgs, 2 * CHIPS - 1, turn_send)
    drain(pw, 2 * PLANE - 1, pw_send)
    drain(pz, NZ - 1, pz_send)
    drain(sol, 2 * PLANE - 1, sol_send)
    drain(planes, NZ - 1, z_send)
    fit_copy.wait_send()


def emit(a_ref, b_ref, c_ref, d_ref, sem):
    copies = [pltpu.make_async_copy(a_ref, c_ref, sem.at[0]), pltpu.make_async_copy(b_ref, d_ref, sem.at[1])]
    for c in copies:
        c.start()
    for c in copies:
        c.wait()


def per_device(samples, fir_coeffs, kept_channels, usable, initial_gains):
    tiles = samples.reshape(4, FRAMES * TILES, 128).transpose(1, 0, 2)
    coeffs = fir_coeffs.reshape(TAPS, TILES, 128).transpose(1, 0, 2)
    chan = kept_channels.reshape(1, KEPT)
    vmem = pl.BlockSpec(memory_space=pltpu.VMEM)
    dma = pltpu.SemaphoreType.DMA
    solved, band = pl.pallas_call(
        kernel,
        name="fx_calibrate",
        out_shape=[jax.ShapeDtypeStruct((2, INPUTS), f32)] * 2,
        in_specs=[pl.BlockSpec(memory_space=pltpu.HBM)] * 5,
        out_specs=[vmem] * 2,
        scratch_shapes=[
            pltpu.VMEM((FRAMES, QT, 4, 4, 128), bf),
            pltpu.VMEM((TILES, TAPS, 128), f32),
            pltpu.VMEM((1, KEPT), jnp.int32),
            pltpu.VMEM((1, INPUTS), jnp.int32),
            pltpu.VMEM((2, INPUTS), f32),
            pltpu.VMEM((16 * SPEC, KC * 128), bf),
            pltpu.VMEM((16 * SPEC, KC * 128), bf),
            pltpu.VMEM((2, KC * 128, KEPT), bf),
            pltpu.VMEM((2, KC * 128, KEPT), bf),
            pltpu.VMEM((4, 16 * SPEC, 128), f32),
            pltpu.VMEM((2, QT, KEPT), f32),
            pltpu.VMEM((2, 128, KEPT), f32),
            pltpu.VMEM((4 * KEPT, 128), f32),
            pltpu.VMEM((2 * CHIPS, 4, 128), bf),
            pltpu.VMEM((2 * CHIPS, 4, 128), bf),
            pltpu.VMEM((2 * PLANE, 8, 128), f32),
            pltpu.VMEM((NZ, 8, 128), f32),
            pltpu.VMEM((2, 8, 128), bf),
            pltpu.VMEM((2 * PLANE, 8, 128), bf),
            pltpu.VMEM((2 * PLANE + 2, POLY, 128), f32),
            pltpu.VMEM((NZ, POLY * 8, 128), bf),
            pltpu.VMEM((2, 8, 128), f32),
            pltpu.VMEM((8, 128), f32),
            dma((CHUNKS, 4)),
            dma((4,)),
        ]
        + [dma] * 13
        + [pltpu.SemaphoreType.REGULAR],
        compiler_params=pltpu.CompilerParams(
            collective_id=0, has_side_effects=True, vmem_limit_bytes=60 * 2**20
        ),
    )(tiles, coeffs, chan, usable.reshape(1, INPUTS), initial_gains.reshape(2, INPUTS))
    solved, band = pl.pallas_call(
        emit,
        name="emit",
        out_shape=[jax.ShapeDtypeStruct((2, INPUTS), f32)] * 2,
        in_specs=[pl.BlockSpec(memory_space=pltpu.HBM)] * 2,
        out_specs=[pl.BlockSpec(memory_space=pltpu.HBM)] * 2,
        scratch_shapes=[dma((2,))],
        compiler_params=pltpu.CompilerParams(vmem_limit_bytes=60 * 2**20),
    )(solved, band)
    return solved.reshape(1, 2, INPUTS), band.reshape(1, 2, INPUTS)


def solution(mesh):
    placed = (P(("grp", "rep"), None), P(), P(), P(), P(("grp", "rep"), None, None))
    return jax.shard_map(
        per_device,
        mesh=mesh,
        in_specs=placed,
        out_specs=(P(("grp", "rep"), None, None), P(("grp", "rep"), None, None)),
        check_vma=False,
    )
```

```python
import math

import jax
import jax.numpy as jnp
from jax import lax
from jax.experimental import pallas as pl
from jax.experimental.pallas import tpu as pltpu
from jax.sharding import PartitionSpec as P

bf, f32 = jnp.bfloat16, jnp.float32
MESH = pl.DeviceIdType.MESH
CHAN = 8192
NFFT = 16384
SPEC = 64
TAPS = 4
FRAMES = SPEC + TAPS - 1
KEPT = 256
INPUTS = 1024
ITERS = 4
POLY = 8
NX, NY, NZ = 4, 4, 8
CHIPS = NX * NY * NZ
PLANE = NX * NY
TILES = NFFT // 128
QT = TILES // 4
KC = 4
EDGE = 2
CHUNKS = (QT - 2 * EDGE) // KC


def turns(phase):
    quad = (phase + NFFT // 8) // (NFFT // 4)
    x = (phase - quad * (NFFT // 4)).astype(f32) * f32(2.0 * math.pi / NFFT)
    x2 = x * x
    s = x * (1.0 + x2 * (-1.0 / 6 + x2 * (1.0 / 120 + x2 * (-1.0 / 5040 + x2 * (1.0 / 362880)))))
    c = 1.0 + x2 * (-0.5 + x2 * (1.0 / 24 + x2 * (-1.0 / 720 + x2 * (1.0 / 40320))))
    odd = (quad & 1) == 1
    cc = jnp.where(odd, s, c)
    ss = jnp.where(odd, c, s)
    cc = jnp.where((quad == 1) | (quad == 2), -cc, cc)
    ss = jnp.where((quad == 2) | (quad == 3), -ss, ss)
    return cc, ss


def far_first(n):
    return sorted(range(n), key=lambda d: -min(d, n - d))


PLANE_ORDER = sorted(
    ((dx, dy) for dx in range(NX) for dy in range(NY)),
    key=lambda d: -min(d[0], NX - d[0]) - min(d[1], NY - d[1]),
)


def loop(f, n):
    def step(i, carry):
        f(i)
        return carry

    lax.fori_loop(0, n, step, 0)


def kernel(
    x_hbm, fir_hbm, chan_hbm, use_hbm, gain_hbm,
    solved_ref, band_ref,
    X, fir_ref, chan_ref, use_ref, gain_ref,
    Fa, Fb, Ta, Tb, acc, hi, lo, wide, msgs, turned,
    pw, pz, mysol, sol, splat, planes, fit, fit_out,
    in_sem, arg_sem, turn_send, turn_recv, self_sem,
    pw_send, pw_recv, pz_send, pz_recv,
    sol_send, sol_recv, z_send, z_recv, fit_send, fit_recv, ready,
):
    g = lax.axis_index("grp")
    r = lax.axis_index("rep")
    z = lax.rem(g, NZ)
    xy = g // NZ
    y = lax.rem(xy, NY)
    x = xy // NY

    src = x_hbm.reshape(FRAMES, 4, QT, 4, 128)

    def sample_copies(k, first, tiles):
        at = pl.ds(first, tiles)
        return [pltpu.make_async_copy(src.at[:, j, at], X.at[:, at, j], in_sem.at[k, j]) for j in range(4)]

    def chunk(k):
        return sample_copies(k + 1, EDGE + KC * k, KC)

    head = sample_copies(0, 0, EDGE)
    tail = sample_copies(CHUNKS + 1, QT - EDGE, EDGE)

    args = [
        pltpu.make_async_copy(a, b, arg_sem.at[i])
        for i, (a, b) in enumerate(
            [(chan_hbm, chan_ref), (fir_hbm, fir_ref), (use_hbm, use_ref), (gain_hbm, gain_ref)]
        )
    ]
    args[0].start()
    args[1].start()
    for copy in sum([head] + [chunk(k) for k in range(CHUNKS)] + [tail], []):
        copy.start()
    args[2].start()
    args[3].start()

    barrier = pltpu.get_barrier_semaphore()

    def greet(chip, core):
        pl.semaphore_signal(barrier, inc=1, device_id=(chip, core), device_id_type=MESH)

    def plane_chips():
        return [lax.rem(x + dx, NX) * NY + lax.rem(y + dy, NY) for dx, dy in PLANE_ORDER]

    for t in plane_chips()[:-1]:
        greet(t * NZ + z, 0)
        greet(t * NZ + z, 1)
    greet(g, 1 - r)
    for d in far_first(NZ)[:-1]:
        greet(xy * NZ + lax.rem(z + d, NZ), r)

    def plane_is_here():
        pl.semaphore_wait(barrier, 2 * PLANE - 1 + NZ - 1)
        for d in far_first(NZ)[:-1]:
            pl.semaphore_signal(
                ready, inc=1, device_id=(xy * NZ + lax.rem(z + d, NZ), r), device_id_type=MESH
            )

    args[0].wait()
    chan = chan_ref[...]

    def table(n0, rows, step):
        n = (lax.broadcasted_iota(jnp.int32, (rows, KEPT), 0) + n0) * step
        return turns((n * chan) & (NFFT - 1))

    c, s = table(0, QT, 128)
    hi[0] = c
    hi[1] = -s

    def low_table(i):
        c, s = table(i * 16, 16, 1)
        at = pl.ds(pl.multiple_of(i * 16, 16), 16)
        lo[0, at, :] = c
        lo[1, at, :] = -s

    loop(low_table, 8)

    rows = X.reshape(FRAMES, QT, 16, 128)
    quarter = lax.broadcasted_iota(jnp.int32, (16, 128), 0) // 4

    def fir(first, h, F, T):
        kk = first + h
        static = isinstance(h, int)
        col = slice(h * 128, h * 128 + 128) if static else pl.ds(pl.multiple_of(h * 128, 128), 128)
        coef = []
        for t in range(TAPS):
            b = [jnp.broadcast_to(fir_ref[j * QT + kk, pl.ds(t, 1)], (16, 128)) for j in range(4)]
            coef.append(
                jnp.where(
                    quarter == 0, b[0], jnp.where(quarter == 1, b[1], jnp.where(quarter == 2, b[2], b[3]))
                )
            )
        w = [rows[f, kk].astype(f32) for f in range(TAPS - 1)]
        for s in range(SPEC):
            w.append(rows[s + TAPS - 1, kk].astype(f32))
            o = coef[0] * w[0] + coef[1] * w[1] + coef[2] * w[2] + coef[3] * w[3]
            F[s * 16 : (s + 1) * 16, col] = o.astype(bf)
            w = w[1:]
        hr, hm = hi[0, pl.ds(kk, 1), :], hi[1, pl.ds(kk, 1), :]
        for q in range(8):
            lr, lm = lo[0, q * 16 : (q + 1) * 16, :], lo[1, q * 16 : (q + 1) * 16, :]
            first = h * 128 + q * 16
            row = slice(first, first + 16) if static else pl.ds(pl.multiple_of(first, 16), 16)
            T[0, row, :] = (hr * lr - hm * lm).astype(bf)
            T[1, row, :] = (hr * lm + hm * lr).astype(bf)

    def mm(F, T, tiles=KC, first=False):
        depth = tiles * 128
        for n in range(2):
            d = jnp.dot(F[:, 0:depth], T[n, 0:depth, :], preferred_element_type=f32)
            for q in range(2):
                if first:
                    acc[2 * n + q] = d[:, q * 128 : (q + 1) * 128]
                else:
                    acc[2 * n + q] += d[:, q * 128 : (q + 1) * 128]

    def wait(copies):
        for copy in copies:
            copy.wait()

    def stage(k, prev, cur, **kw):
        wait(chunk(k))
        mm(*prev, **kw)
        for h in range(KC):
            fir(EDGE + KC * k, h, *cur)

    A, B = (Fa, Ta), (Fb, Tb)
    args[1].wait()
    wait(head)
    loop(lambda h: fir(0, h, *A), EDGE)
    stage(0, A, B, tiles=EDGE, first=True)

    def pair(i):
        pl.when(i == CHUNKS // 2 - 2)(plane_is_here)
        stage(2 * i + 1, B, A)
        stage(2 * i + 2, A, B)

    loop(pair, CHUNKS // 2)
    wait(tail)
    mm(*B)
    for h in range(EDGE):
        fir(QT - EDGE, h, *A)
    mm(*A, tiles=EDGE)

    quads = []
    for j in range(4):
        ph = (chan * j) & 3
        rr = jnp.where(ph == 0, 1.0, jnp.where(ph == 2, -1.0, 0.0))
        ri = jnp.where(ph == 1, -1.0, jnp.where(ph == 3, 1.0, 0.0))
        quads.append((rr, ri))
    sub8 = lax.broadcasted_iota(jnp.int32, (8, 128), 0)
    lane8 = lax.broadcasted_iota(jnp.int32, (8, 128), 1)
    power_row, power_lane = xy // 2, lax.rem(xy, 2) * 64 + z * 8 + r * 4
    powers = jnp.zeros((8, 128), f32)
    spectra = []
    for p in range(4):
        sr = si = None
        for j in range(4):
            rr, ri = quads[j]
            at = pl.ds(j * 4 + p, SPEC, stride=16)
            a, b = [jnp.concatenate([acc[q, at, :], acc[q + 1, at, :]], axis=1) for q in (0, 2)]
            tr = rr * a - ri * b if j else a
            ti = rr * b + ri * a if j else b
            sr = tr if sr is None else sr + tr
            si = ti if si is None else si + ti
        v = jnp.concatenate([sr, si], axis=0)
        q = v.astype(bf).astype(f32)
        power = jnp.sum(jnp.sum(q * q, axis=1, keepdims=True), axis=0, keepdims=True)
        powers = jnp.where((sub8 == power_row) & (lane8 == power_lane + p), power, powers)
        spectra.append(v)
    pz[z] = powers * f32(1.0 / (SPEC * KEPT))
    pl.semaphore_wait(ready, NZ - 1)

    def send_plane(source, buf, send, recv):
        def one(chip, core):
            pltpu.make_async_remote_copy(
                src_ref=source(core), dst_ref=buf.at[xy * 2 + r], send_sem=send, recv_sem=recv,
                device_id=(chip, core), device_id_type=MESH,
            ).start()

        for t in plane_chips()[:-1]:
            one(t * NZ + z, 0)
            one(t * NZ + z, 1)
        one(g, 1 - r)

    def send_z(buf, send, recv):
        for d in far_first(NZ)[:-1]:
            pltpu.make_async_remote_copy(
                src_ref=buf.at[z], dst_ref=buf.at[z], send_sem=send, recv_sem=recv,
                device_id=(xy * NZ + lax.rem(z + d, NZ), r), device_id_type=MESH,
            ).start()

    def drain(buf, n, sem):
        pltpu.make_async_copy(buf.at[pl.ds(0, n)], buf.at[pl.ds(0, n)], sem).wait()

    send_z(pz, pz_send, pz_recv)

    for p in range(4):
        wide[pl.ds(p, KEPT, stride=4), :] = spectra[p].T
    msgs.reshape(KEPT * 4, 128)[...] = wide[...].astype(bf)
    me = 2 * g + r

    def send_block(t):
        pltpu.make_async_remote_copy(
            src_ref=msgs.at[t], dst_ref=turned.at[me], send_sem=turn_send, recv_sem=turn_recv,
            device_id=(t // 2, lax.rem(t, 2)), device_id_type=MESH,
        ).start()

    def send_chip(t):
        for core in range(2):
            pltpu.make_async_remote_copy(
                src_ref=msgs.at[2 * t + core], dst_ref=turned.at[me], send_sem=turn_send, recv_sem=turn_recv,
                device_id=(t, core), device_id_type=MESH,
            ).start()

    def send_level(k):
        far = lax.rem(z + NZ // 2 + (1 - 2 * lax.rem(k, 2)) * ((k + 1) // 2), NZ)
        for m in range(PLANE):
            send_chip(lax.rem(xy + PLANE // 2 + m, PLANE) * NZ + far)

    loop(send_level, NZ - 2)

    drain(pz, NZ - 1, pz_recv)
    t = pz[0]
    for i in range(1, NZ):
        t = t + pz[i]
    pw[xy * 2 + r] = t
    send_plane(lambda core: pw.at[xy * 2 + r], pw, pw_send, pw_recv)

    send_level(NZ - 2)
    for m in range(1, PLANE):
        send_chip(lax.rem(xy + m, PLANE) * NZ + z)
    send_block(2 * g + 1 - r)
    self_copy = pltpu.make_async_copy(msgs.at[me], turned.at[me], self_sem)
    self_copy.start()

    u = chan.astype(f32) * f32(2.0 / (CHAN - 1)) - 1.0
    poly = [jnp.ones_like(u), u]
    for order in range(1, POLY - 1):
        poly.append(((2 * order + 1) * u * poly[order] - order * poly[order - 1]) / (order + 1))
    sub = lax.broadcasted_iota(jnp.int32, (POLY, KEPT), 0)
    basis = jnp.zeros((POLY, KEPT), f32)
    for k in range(POLY):
        basis = jnp.where(sub == k, jnp.broadcast_to(poly[k], (POLY, KEPT)), basis)
    lane = lax.broadcasted_iota(jnp.int32, (POLY, KEPT), 1)

    def column(q):
        return jnp.sum(jnp.where(lane == q, basis, 0.0), axis=1, keepdims=True)

    aug = jnp.zeros((POLY, 128), f32)
    for k in range(POLY):
        aug = jnp.where(lane8 == k, jnp.sum(basis * poly[k], axis=1, keepdims=True), aug)
    aug = jnp.where(lane8 == POLY, column(2 * g + r), aug)
    aug = jnp.where(lane8 == POLY + 1, column(2 * g + 1 - r), aug)
    for k in range(POLY):
        pivot_row = jnp.sum(jnp.where(sub8 == k, aug, 0.0), axis=0, keepdims=True)
        pivot = jnp.sum(jnp.where(lane8[0:1] == k, pivot_row, 0.0), axis=1, keepdims=True)
        pivot_row = pivot_row / pivot
        factor = jnp.sum(jnp.where(lane8 == k, aug, 0.0), axis=1, keepdims=True)
        aug = jnp.where(sub8 == k, pivot_row, aug - factor * pivot_row)
    for i in range(2):
        v = jnp.sum(jnp.where(lane8 == POLY + i, aug, 0.0), axis=1, keepdims=True)
        splat[2 * PLANE + i] = jnp.broadcast_to(v, (POLY, 128))
    for i in range(2 * PLANE):
        splat[i] = jnp.broadcast_to(column(i // 2 * (2 * NZ) + z * 2 + i % 2), (POLY, 128))

    drain(pw, 2 * PLANE - 1, pw_recv)
    t = pw[0]
    for i in range(1, 2 * PLANE):
        t = t + pw[i]
    t = lax.rsqrt(t + f32(1e-06))
    scale = jnp.concatenate([t[j : j + 1, :] for j in range(8)], axis=1)

    args[2].wait()
    args[3].wait()
    self_copy.wait()
    drain(turned, 2 * CHIPS - 1, turn_recv)

    eye = (
        lax.broadcasted_iota(jnp.int32, (128, 128), 0) == lax.broadcasted_iota(jnp.int32, (128, 128), 1)
    ).astype(f32).astype(bf)
    cols = lax.dot_general(
        eye, turned.reshape(INPUTS, 128)[...], (((1,), (1,)), ((), ())), preferred_element_type=f32
    )
    xr, xi = cols[0:SPEC], cols[SPEC : 2 * SPEC]
    use = use_ref[...].astype(f32)
    scale = scale * use
    gr, gi = gain_ref[0:1, :], gain_ref[1:2, :]
    for step in range(ITERS):
        ar, ai = gr * scale, gi * scale
        zr = xr * ar - xi * ai
        zi = xr * ai + xi * ar
        dr = jnp.sum(zr, axis=1, keepdims=True) - zr
        di = jnp.sum(zi, axis=1, keepdims=True) - zi
        nr = jnp.sum(xr * dr + xi * di, axis=0, keepdims=True) * f32(1.0 / SPEC) * scale
        ni = jnp.sum(xr * di - xi * dr, axis=0, keepdims=True) * f32(1.0 / SPEC) * scale
        mag = use * (gr * gr + gi * gi)
        denom = jnp.sum(mag, axis=1, keepdims=True) - mag + f32(1e-06)
        fr, fi = nr / denom, ni / denom
        if step % 2 == 1:
            gr, gi = (fr + gr) * 0.5, (fi + gi) * 0.5
        else:
            gr, gi = fr, fi
    solved_ref[0:1, :] = gr
    solved_ref[1:2, :] = gi
    for i, v in enumerate((gr, gi)):
        t = jnp.zeros((8, 128), f32)
        for j in range(8):
            t = jnp.where(sub8 == j, jnp.broadcast_to(v[:, j * 128 : (j + 1) * 128], (8, 128)), t)
        mysol[i] = t.astype(bf)

    send_plane(lambda core: mysol.at[core], sol, sol_send, sol_recv)
    sol[xy * 2 + r] = mysol[r]
    drain(sol, 2 * PLANE - 1, sol_recv)
    part = []
    for k in range(POLY):
        m = None
        for i in range(2 * PLANE):
            t = sol[i].astype(f32) * splat[i, k : k + 1, :]
            m = t if m is None else m + t
        part.append(m)
    part = jnp.concatenate(part, axis=0)
    sent = part.astype(bf)
    planes[z] = sent
    send_z(planes, z_send, z_recv)
    total = part - sent.astype(f32)
    drain(planes, NZ - 1, z_recv)
    for i in range(NZ):
        total = total + planes[i].astype(f32)
    mine = theirs = None
    for k in range(POLY):
        m = total[8 * k : 8 * (k + 1)]
        a, b = m * splat[2 * PLANE, k : k + 1, :], m * splat[2 * PLANE + 1, k : k + 1, :]
        mine = a if mine is None else mine + a
        theirs = b if theirs is None else theirs + b
    fit_out[...] = theirs
    fit_copy = pltpu.make_async_remote_copy(
        src_ref=fit_out, dst_ref=fit.at[r], send_sem=fit_send, recv_sem=fit_recv,
        device_id=(g, 1 - r), device_id_type=MESH,
    )
    fit_copy.start()
    fit[r] = mine
    fit_copy.wait_recv()
    for i in range(2):
        for j in range(8):
            band_ref[i : i + 1, j * 128 : (j + 1) * 128] = fit[i, j : j + 1, :]

    drain(msgs, 2 * CHIPS - 1, turn_send)
    drain(pw, 2 * PLANE - 1, pw_send)
    drain(pz, NZ - 1, pz_send)
    drain(sol, 2 * PLANE - 1, sol_send)
    drain(planes, NZ - 1, z_send)
    fit_copy.wait_send()


def emit(a_ref, b_ref, c_ref, d_ref, sem):
    copies = [pltpu.make_async_copy(a_ref, c_ref, sem.at[0]), pltpu.make_async_copy(b_ref, d_ref, sem.at[1])]
    for c in copies:
        c.start()
    for c in copies:
        c.wait()


def per_device(samples, fir_coeffs, kept_channels, usable, initial_gains):
    tiles = samples.reshape(4, FRAMES * TILES, 128).transpose(1, 0, 2)
    coeffs = fir_coeffs.reshape(TAPS, TILES, 128).transpose(1, 0, 2)
    chan = kept_channels.reshape(1, KEPT)
    vmem = pl.BlockSpec(memory_space=pltpu.VMEM)
    dma = pltpu.SemaphoreType.DMA
    solved, band = pl.pallas_call(
        kernel,
        name="fx_calibrate",
        out_shape=[pltpu.VMEM((2, INPUTS), f32)] * 2,
        in_specs=[pl.BlockSpec(memory_space=pltpu.HBM)] * 5,
        out_specs=[vmem] * 2,
        scratch_shapes=[
            pltpu.VMEM((FRAMES, QT, 4, 4, 128), bf),
            pltpu.VMEM((TILES, TAPS, 128), f32),
            pltpu.VMEM((1, KEPT), jnp.int32),
            pltpu.VMEM((1, INPUTS), jnp.int32),
            pltpu.VMEM((2, INPUTS), f32),
            pltpu.VMEM((16 * SPEC, KC * 128), bf),
            pltpu.VMEM((16 * SPEC, KC * 128), bf),
            pltpu.VMEM((2, KC * 128, KEPT), bf),
            pltpu.VMEM((2, KC * 128, KEPT), bf),
            pltpu.VMEM((4, 16 * SPEC, 128), f32),
            pltpu.VMEM((2, QT, KEPT), f32),
            pltpu.VMEM((2, 128, KEPT), f32),
            pltpu.VMEM((4 * KEPT, 128), f32),
            pltpu.VMEM((2 * CHIPS, 4, 128), bf),
            pltpu.VMEM((2 * CHIPS, 4, 128), bf),
            pltpu.VMEM((2 * PLANE, 8, 128), f32),
            pltpu.VMEM((NZ, 8, 128), f32),
            pltpu.VMEM((2, 8, 128), bf),
            pltpu.VMEM((2 * PLANE, 8, 128), bf),
            pltpu.VMEM((2 * PLANE + 2, POLY, 128), f32),
            pltpu.VMEM((NZ, POLY * 8, 128), bf),
            pltpu.VMEM((2, 8, 128), f32),
            pltpu.VMEM((8, 128), f32),
            dma((CHUNKS + 2, 4)),
            dma((4,)),
        ]
        + [dma] * 13
        + [pltpu.SemaphoreType.REGULAR],
        compiler_params=pltpu.CompilerParams(
            collective_id=0, has_side_effects=True, vmem_limit_bytes=60 * 2**20
        ),
    )(tiles, coeffs, chan, usable.reshape(1, INPUTS), initial_gains.reshape(2, INPUTS))
    solved, band = pl.pallas_call(
        emit,
        name="emit",
        out_shape=[jax.ShapeDtypeStruct((2, INPUTS), f32)] * 2,
        in_specs=[pl.BlockSpec(memory_space=pltpu.VMEM)] * 2,
        out_specs=[pl.BlockSpec(memory_space=pltpu.HBM)] * 2,
        scratch_shapes=[dma((2,))],
        compiler_params=pltpu.CompilerParams(vmem_limit_bytes=2**20),
    )(solved, band)
    return solved.reshape(1, 2, INPUTS), band.reshape(1, 2, INPUTS)


def solution(mesh):
    placed = (P(("grp", "rep"), None), P(), P(), P(), P(("grp", "rep"), None, None))
    return jax.shard_map(
        per_device,
        mesh=mesh,
        in_specs=placed,
        out_specs=(P(("grp", "rep"), None, None), P(("grp", "rep"), None, None)),
        check_vma=False,
    )
```

```python
import math

import jax
import jax.numpy as jnp
from jax import lax
from jax.experimental import pallas as pl
from jax.experimental.pallas import tpu as pltpu
from jax.sharding import PartitionSpec as P

bf, f32 = jnp.bfloat16, jnp.float32
MESH = pl.DeviceIdType.MESH
CHAN = 8192
NFFT = 16384
SPEC = 64
TAPS = 4
FRAMES = SPEC + TAPS - 1
KEPT = 256
INPUTS = 1024
ITERS = 4
POLY = 8
NX, NY, NZ = 4, 4, 8
CHIPS = NX * NY * NZ
PLANE = NX * NY
TILES = NFFT // 128
QT = TILES // 4
KC = 4
EDGE = 2
CHUNKS = (QT - 2 * EDGE) // KC


def turns(phase):
    quad = (phase + NFFT // 8) // (NFFT // 4)
    x = (phase - quad * (NFFT // 4)).astype(f32) * f32(2.0 * math.pi / NFFT)
    x2 = x * x
    s = x * (1.0 + x2 * (-1.0 / 6 + x2 * (1.0 / 120 + x2 * (-1.0 / 5040 + x2 * (1.0 / 362880)))))
    c = 1.0 + x2 * (-0.5 + x2 * (1.0 / 24 + x2 * (-1.0 / 720 + x2 * (1.0 / 40320))))
    odd = (quad & 1) == 1
    cc = jnp.where(odd, s, c)
    ss = jnp.where(odd, c, s)
    cc = jnp.where((quad == 1) | (quad == 2), -cc, cc)
    ss = jnp.where((quad == 2) | (quad == 3), -ss, ss)
    return cc, ss


def far_first(n):
    return sorted(range(n), key=lambda d: -min(d, n - d))


PLANE_ORDER = sorted(
    ((dx, dy) for dx in range(NX) for dy in range(NY)),
    key=lambda d: -min(d[0], NX - d[0]) - min(d[1], NY - d[1]),
)


def loop(f, n):
    def step(i, carry):
        f(i)
        return carry

    lax.fori_loop(0, n, step, 0)


def kernel(
    x_hbm, fir_hbm, chan_hbm, use_hbm, gain_hbm,
    solved_ref, band_ref,
    X, fir_ref, chan_ref, use_ref, gain_ref,
    Fa, Fb, Ta, Tb, acc, hi, lo, wide, msgs, turned,
    pw, pz, mysol, sol, splat, planes, fit, fit_out,
    in_sem, arg_sem, turn_send, turn_recv, self_sem,
    pw_send, pw_recv, pz_send, pz_recv,
    sol_send, sol_recv, z_send, z_recv, fit_send, fit_recv, ready,
):
    g = lax.axis_index("grp")
    r = lax.axis_index("rep")
    z = lax.rem(g, NZ)
    xy = g // NZ
    y = lax.rem(xy, NY)
    x = xy // NY

    src = x_hbm.reshape(FRAMES, 4, QT, 4, 128)

    def sample_copies(k, first, tiles):
        at = pl.ds(first, tiles)
        return [pltpu.make_async_copy(src.at[:, j, at], X.at[:, at, j], in_sem.at[k, j]) for j in range(4)]

    def chunk(k):
        return sample_copies(k + 1, EDGE + KC * k, KC)

    head = sample_copies(0, 0, EDGE)
    tail = sample_copies(CHUNKS + 1, QT - EDGE, EDGE)

    args = [
        pltpu.make_async_copy(a, b, arg_sem.at[i])
        for i, (a, b) in enumerate(
            [(chan_hbm, chan_ref), (fir_hbm, fir_ref), (use_hbm, use_ref), (gain_hbm, gain_ref)]
        )
    ]
    args[0].start()
    args[1].start()
    for copy in sum([head] + [chunk(k) for k in range(CHUNKS)] + [tail], []):
        copy.start()
    args[2].start()
    args[3].start()

    barrier = pltpu.get_barrier_semaphore()

    def greet(chip, core):
        pl.semaphore_signal(barrier, inc=1, device_id=(chip, core), device_id_type=MESH)

    def plane_chips():
        return [lax.rem(x + dx, NX) * NY + lax.rem(y + dy, NY) for dx, dy in PLANE_ORDER]

    for t in plane_chips()[:-1]:
        greet(t * NZ + z, 0)
        greet(t * NZ + z, 1)
    greet(g, 1 - r)
    for d in far_first(NZ)[:-1]:
        greet(xy * NZ + lax.rem(z + d, NZ), r)

    def plane_is_here():
        pl.semaphore_wait(barrier, 2 * PLANE - 1 + NZ - 1)
        for d in far_first(NZ)[:-1]:
            pl.semaphore_signal(
                ready, inc=1, device_id=(xy * NZ + lax.rem(z + d, NZ), r), device_id_type=MESH
            )

    args[0].wait()
    chan = chan_ref[...]

    def table(n0, rows, step):
        n = (lax.broadcasted_iota(jnp.int32, (rows, KEPT), 0) + n0) * step
        return turns((n * chan) & (NFFT - 1))

    c, s = table(0, QT, 128)
    hi[0] = c
    hi[1] = -s

    def low_table(i):
        c, s = table(i * 16, 16, 1)
        at = pl.ds(pl.multiple_of(i * 16, 16), 16)
        lo[0, at, :] = c
        lo[1, at, :] = -s

    loop(low_table, 8)

    rows = X.reshape(FRAMES, QT, 16, 128)
    quarter = lax.broadcasted_iota(jnp.int32, (16, 128), 0) // 4

    def fir(first, h, F, T):
        kk = first + h
        static = isinstance(h, int)
        col = slice(h * 128, h * 128 + 128) if static else pl.ds(pl.multiple_of(h * 128, 128), 128)
        coef = []
        for t in range(TAPS):
            b = [jnp.broadcast_to(fir_ref[j * QT + kk, pl.ds(t, 1)], (16, 128)) for j in range(4)]
            coef.append(
                jnp.where(
                    quarter == 0, b[0], jnp.where(quarter == 1, b[1], jnp.where(quarter == 2, b[2], b[3]))
                )
            )
        w = [rows[f, kk].astype(f32) for f in range(TAPS - 1)]
        for s in range(SPEC):
            w.append(rows[s + TAPS - 1, kk].astype(f32))
            o = coef[0] * w[0] + coef[1] * w[1] + coef[2] * w[2] + coef[3] * w[3]
            F[s * 16 : (s + 1) * 16, col] = o.astype(bf)
            w = w[1:]
        hr, hm = hi[0, pl.ds(kk, 1), :], hi[1, pl.ds(kk, 1), :]
        for q in range(8):
            lr, lm = lo[0, q * 16 : (q + 1) * 16, :], lo[1, q * 16 : (q + 1) * 16, :]
            first = h * 128 + q * 16
            row = slice(first, first + 16) if static else pl.ds(pl.multiple_of(first, 16), 16)
            T[0, row, :] = (hr * lr - hm * lm).astype(bf)
            T[1, row, :] = (hr * lm + hm * lr).astype(bf)

    def mm(F, T, tiles=KC, first=False):
        depth = tiles * 128
        for n in range(2):
            d = jnp.dot(F[:, 0:depth], T[n, 0:depth, :], preferred_element_type=f32)
            for q in range(2):
                if first:
                    acc[2 * n + q] = d[:, q * 128 : (q + 1) * 128]
                else:
                    acc[2 * n + q] += d[:, q * 128 : (q + 1) * 128]

    def wait(copies):
        for copy in copies:
            copy.wait()

    def stage(k, prev, cur, **kw):
        wait(chunk(k))
        mm(*prev, **kw)
        for h in range(KC):
            fir(EDGE + KC * k, h, *cur)

    A, B = (Fa, Ta), (Fb, Tb)
    args[1].wait()
    wait(head)
    loop(lambda h: fir(0, h, *A), EDGE)
    stage(0, A, B, tiles=EDGE, first=True)

    def pair(i):
        pl.when(i == CHUNKS // 2 - 2)(plane_is_here)
        stage(2 * i + 1, B, A)
        stage(2 * i + 2, A, B)

    loop(pair, CHUNKS // 2)
    wait(tail)
    mm(*B)
    for h in range(EDGE):
        fir(QT - EDGE, h, *A)
    mm(*A, tiles=EDGE)

    quads = []
    for j in range(4):
        ph = (chan * j) & 3
        rr = jnp.where(ph == 0, 1.0, jnp.where(ph == 2, -1.0, 0.0))
        ri = jnp.where(ph == 1, -1.0, jnp.where(ph == 3, 1.0, 0.0))
        quads.append((rr, ri))
    sub8 = lax.broadcasted_iota(jnp.int32, (8, 128), 0)
    lane8 = lax.broadcasted_iota(jnp.int32, (8, 128), 1)
    power_lane = lax.rem(xy, 2) * 64 + z * 8 + r * 4
    powers = jnp.zeros((1, 128), f32)
    spectra = []
    for p in range(4):
        sr = si = None
        for j in range(4):
            rr, ri = quads[j]
            at = pl.ds(j * 4 + p, SPEC, stride=16)
            a, b = [jnp.concatenate([acc[q, at, :], acc[q + 1, at, :]], axis=1) for q in (0, 2)]
            tr = rr * a - ri * b if j else a
            ti = rr * b + ri * a if j else b
            sr = tr if sr is None else sr + tr
            si = ti if si is None else si + ti
        v = jnp.concatenate([sr, si], axis=0)
        q = v.astype(bf).astype(f32)
        power = jnp.sum(jnp.sum(q * q, axis=1, keepdims=True), axis=0, keepdims=True)
        powers = jnp.where(lane8[0:1] == power_lane + p, power, powers)
        spectra.append(v)
    pz[z] = powers * f32(1.0 / (SPEC * KEPT))
    pl.semaphore_wait(ready, NZ - 1)

    def send_plane(source, buf, send, recv):
        def one(chip, core):
            pltpu.make_async_remote_copy(
                src_ref=source(core), dst_ref=buf.at[xy * 2 + r], send_sem=send, recv_sem=recv,
                device_id=(chip, core), device_id_type=MESH,
            ).start()

        for t in plane_chips()[:-1]:
            one(t * NZ + z, 0)
            one(t * NZ + z, 1)
        one(g, 1 - r)

    def send_z(buf, send, recv):
        for d in far_first(NZ)[:-1]:
            pltpu.make_async_remote_copy(
                src_ref=buf.at[z], dst_ref=buf.at[z], send_sem=send, recv_sem=recv,
                device_id=(xy * NZ + lax.rem(z + d, NZ), r), device_id_type=MESH,
            ).start()

    def drain(buf, n, sem):
        pltpu.make_async_copy(buf.at[pl.ds(0, n)], buf.at[pl.ds(0, n)], sem).wait()

    send_z(pz, pz_send, pz_recv)

    for p in range(4):
        wide[pl.ds(p, KEPT, stride=4), :] = spectra[p].T
    msgs.reshape(KEPT * 4, 128)[...] = wide[...].astype(bf)
    me = 2 * g + r

    def send_block(t):
        pltpu.make_async_remote_copy(
            src_ref=msgs.at[t], dst_ref=turned.at[me], send_sem=turn_send, recv_sem=turn_recv,
            device_id=(t // 2, lax.rem(t, 2)), device_id_type=MESH,
        ).start()

    def send_chip(t):
        for core in range(2):
            pltpu.make_async_remote_copy(
                src_ref=msgs.at[2 * t + core], dst_ref=turned.at[me], send_sem=turn_send, recv_sem=turn_recv,
                device_id=(t, core), device_id_type=MESH,
            ).start()

    def send_level(k):
        far = lax.rem(z + NZ // 2 + (1 - 2 * lax.rem(k, 2)) * ((k + 1) // 2), NZ)
        for m in range(PLANE):
            send_chip(lax.rem(xy + PLANE // 2 + m, PLANE) * NZ + far)

    loop(send_level, NZ - 2)

    drain(pz, NZ - 1, pz_recv)
    t = pz[0]
    for i in range(1, NZ):
        t = t + pz[i]
    pw[xy * 2 + r] = t
    send_plane(lambda core: pw.at[xy * 2 + r], pw, pw_send, pw_recv)

    send_level(NZ - 2)
    for m in range(1, PLANE):
        send_chip(lax.rem(xy + m, PLANE) * NZ + z)
    send_block(2 * g + 1 - r)
    self_copy = pltpu.make_async_copy(msgs.at[me], turned.at[me], self_sem)
    self_copy.start()

    u = chan.astype(f32) * f32(2.0 / (CHAN - 1)) - 1.0
    poly = [jnp.ones_like(u), u]
    for order in range(1, POLY - 1):
        poly.append(((2 * order + 1) * u * poly[order] - order * poly[order - 1]) / (order + 1))
    sub = lax.broadcasted_iota(jnp.int32, (POLY, KEPT), 0)
    basis = jnp.zeros((POLY, KEPT), f32)
    for k in range(POLY):
        basis = jnp.where(sub == k, jnp.broadcast_to(poly[k], (POLY, KEPT)), basis)
    lane = lax.broadcasted_iota(jnp.int32, (POLY, KEPT), 1)

    def column(q):
        return jnp.sum(jnp.where(lane == q, basis, 0.0), axis=1, keepdims=True)

    aug = jnp.zeros((POLY, 128), f32)
    for k in range(POLY):
        aug = jnp.where(lane8 == k, jnp.sum(basis * poly[k], axis=1, keepdims=True), aug)
    aug = jnp.where(lane8 == POLY, column(2 * g + r), aug)
    aug = jnp.where(lane8 == POLY + 1, column(2 * g + 1 - r), aug)
    for k in range(POLY):
        pivot_row = jnp.sum(jnp.where(sub8 == k, aug, 0.0), axis=0, keepdims=True)
        pivot = jnp.sum(jnp.where(lane8[0:1] == k, pivot_row, 0.0), axis=1, keepdims=True)
        pivot_row = pivot_row / pivot
        factor = jnp.sum(jnp.where(lane8 == k, aug, 0.0), axis=1, keepdims=True)
        aug = jnp.where(sub8 == k, pivot_row, aug - factor * pivot_row)
    for i in range(2):
        v = jnp.sum(jnp.where(lane8 == POLY + i, aug, 0.0), axis=1, keepdims=True)
        splat[2 * PLANE + i] = jnp.broadcast_to(v, (POLY, 128))
    for i in range(2 * PLANE):
        splat[i] = jnp.broadcast_to(column(i // 2 * (2 * NZ) + z * 2 + i % 2), (POLY, 128))

    drain(pw, 2 * PLANE - 1, pw_recv)
    scale = jnp.concatenate([pw[4 * j] + pw[4 * j + 1] + pw[4 * j + 2] + pw[4 * j + 3] for j in range(8)], axis=1)
    scale = lax.rsqrt(scale + f32(1e-06))

    args[2].wait()
    args[3].wait()
    self_copy.wait()
    drain(turned, 2 * CHIPS - 1, turn_recv)

    eye = (
        lax.broadcasted_iota(jnp.int32, (128, 128), 0) == lax.broadcasted_iota(jnp.int32, (128, 128), 1)
    ).astype(f32).astype(bf)
    cols = lax.dot_general(
        eye, turned.reshape(INPUTS, 128)[...], (((1,), (1,)), ((), ())), preferred_element_type=f32
    )
    xr, xi = cols[0:SPEC], cols[SPEC : 2 * SPEC]
    use = use_ref[...].astype(f32)
    scale = scale * use
    gr, gi = gain_ref[0:1, :], gain_ref[1:2, :]
    for step in range(ITERS):
        ar, ai = gr * scale, gi * scale
        zr = xr * ar - xi * ai
        zi = xr * ai + xi * ar
        dr = jnp.sum(zr, axis=1, keepdims=True) - zr
        di = jnp.sum(zi, axis=1, keepdims=True) - zi
        nr = jnp.sum(xr * dr + xi * di, axis=0, keepdims=True) * f32(1.0 / SPEC) * scale
        ni = jnp.sum(xr * di - xi * dr, axis=0, keepdims=True) * f32(1.0 / SPEC) * scale
        mag = use * (gr * gr + gi * gi)
        denom = jnp.sum(mag, axis=1, keepdims=True) - mag + f32(1e-06)
        fr, fi = nr / denom, ni / denom
        if step % 2 == 1:
            gr, gi = (fr + gr) * 0.5, (fi + gi) * 0.5
        else:
            gr, gi = fr, fi
    solved_ref[0:1, :] = gr
    solved_ref[1:2, :] = gi
    for i, v in enumerate((gr, gi)):
        t = jnp.zeros((8, 128), f32)
        for j in range(8):
            t = jnp.where(sub8 == j, jnp.broadcast_to(v[:, j * 128 : (j + 1) * 128], (8, 128)), t)
        mysol[i] = t.astype(bf)

    send_plane(lambda core: mysol.at[core], sol, sol_send, sol_recv)
    sol[xy * 2 + r] = mysol[r]
    drain(sol, 2 * PLANE - 1, sol_recv)
    part = []
    for k in range(POLY):
        m = None
        for i in range(2 * PLANE):
            t = sol[i].astype(f32) * splat[i, k : k + 1, :]
            m = t if m is None else m + t
        part.append(m)
    part = jnp.concatenate(part, axis=0)
    sent = part.astype(bf)
    planes[z] = sent
    send_z(planes, z_send, z_recv)
    total = part - sent.astype(f32)
    drain(planes, NZ - 1, z_recv)
    for i in range(NZ):
        total = total + planes[i].astype(f32)
    mine = theirs = None
    for k in range(POLY):
        m = total[8 * k : 8 * (k + 1)]
        a, b = m * splat[2 * PLANE, k : k + 1, :], m * splat[2 * PLANE + 1, k : k + 1, :]
        mine = a if mine is None else mine + a
        theirs = b if theirs is None else theirs + b
    fit_out[...] = theirs
    fit_copy = pltpu.make_async_remote_copy(
        src_ref=fit_out, dst_ref=fit.at[r], send_sem=fit_send, recv_sem=fit_recv,
        device_id=(g, 1 - r), device_id_type=MESH,
    )
    fit_copy.start()
    fit[r] = mine
    fit_copy.wait_recv()
    for i in range(2):
        for j in range(8):
            band_ref[i : i + 1, j * 128 : (j + 1) * 128] = fit[i, j : j + 1, :]

    drain(msgs, 2 * CHIPS - 1, turn_send)
    drain(pw, 2 * PLANE - 1, pw_send)
    drain(pz, NZ - 1, pz_send)
    drain(sol, 2 * PLANE - 1, sol_send)
    drain(planes, NZ - 1, z_send)
    fit_copy.wait_send()


def emit(a_ref, b_ref, c_ref, d_ref, sem):
    copies = [pltpu.make_async_copy(a_ref, c_ref, sem.at[0]), pltpu.make_async_copy(b_ref, d_ref, sem.at[1])]
    for c in copies:
        c.start()
    for c in copies:
        c.wait()


def per_device(samples, fir_coeffs, kept_channels, usable, initial_gains):
    tiles = samples.reshape(4, FRAMES * TILES, 128).transpose(1, 0, 2)
    coeffs = fir_coeffs.reshape(TAPS, TILES, 128).transpose(1, 0, 2)
    chan = kept_channels.reshape(1, KEPT)
    vmem = pl.BlockSpec(memory_space=pltpu.VMEM)
    dma = pltpu.SemaphoreType.DMA
    solved, band = pl.pallas_call(
        kernel,
        name="fx_calibrate",
        out_shape=[pltpu.VMEM((2, INPUTS), f32)] * 2,
        in_specs=[pl.BlockSpec(memory_space=pltpu.HBM)] * 5,
        out_specs=[vmem] * 2,
        scratch_shapes=[
            pltpu.VMEM((FRAMES, QT, 4, 4, 128), bf),
            pltpu.VMEM((TILES, TAPS, 128), f32),
            pltpu.VMEM((1, KEPT), jnp.int32),
            pltpu.VMEM((1, INPUTS), jnp.int32),
            pltpu.VMEM((2, INPUTS), f32),
            pltpu.VMEM((16 * SPEC, KC * 128), bf),
            pltpu.VMEM((16 * SPEC, KC * 128), bf),
            pltpu.VMEM((2, KC * 128, KEPT), bf),
            pltpu.VMEM((2, KC * 128, KEPT), bf),
            pltpu.VMEM((4, 16 * SPEC, 128), f32),
            pltpu.VMEM((2, QT, KEPT), f32),
            pltpu.VMEM((2, 128, KEPT), f32),
            pltpu.VMEM((4 * KEPT, 128), f32),
            pltpu.VMEM((2 * CHIPS, 4, 128), bf),
            pltpu.VMEM((2 * CHIPS, 4, 128), bf),
            pltpu.VMEM((2 * PLANE, 1, 128), f32),
            pltpu.VMEM((NZ, 1, 128), f32),
            pltpu.VMEM((2, 8, 128), bf),
            pltpu.VMEM((2 * PLANE, 8, 128), bf),
            pltpu.VMEM((2 * PLANE + 2, POLY, 128), f32),
            pltpu.VMEM((NZ, POLY * 8, 128), bf),
            pltpu.VMEM((2, 8, 128), f32),
            pltpu.VMEM((8, 128), f32),
            dma((CHUNKS + 2, 4)),
            dma((4,)),
        ]
        + [dma] * 13
        + [pltpu.SemaphoreType.REGULAR],
        compiler_params=pltpu.CompilerParams(
            collective_id=0, has_side_effects=True, vmem_limit_bytes=60 * 2**20
        ),
    )(tiles, coeffs, chan, usable.reshape(1, INPUTS), initial_gains.reshape(2, INPUTS))
    solved, band = pl.pallas_call(
        emit,
        name="emit",
        out_shape=[jax.ShapeDtypeStruct((2, INPUTS), f32)] * 2,
        in_specs=[pl.BlockSpec(memory_space=pltpu.VMEM)] * 2,
        out_specs=[pl.BlockSpec(memory_space=pltpu.HBM)] * 2,
        scratch_shapes=[dma((2,))],
        compiler_params=pltpu.CompilerParams(vmem_limit_bytes=2**20),
    )(solved, band)
    return solved.reshape(1, 2, INPUTS), band.reshape(1, 2, INPUTS)


def solution(mesh):
    placed = (P(("grp", "rep"), None), P(), P(), P(), P(("grp", "rep"), None, None))
    return jax.shard_map(
        per_device,
        mesh=mesh,
        in_specs=placed,
        out_specs=(P(("grp", "rep"), None, None), P(("grp", "rep"), None, None)),
        check_vma=False,
    )
```
